128 devices in a mesh: dp: 16 (over x_hi, z, core), row: 2 (over x_lo), col: 4 (over y).
Axes of the slice: x: 4 (x_hi: 2, x_lo: 2; x = x_hi * 2 + x_lo), y: 4, z: 4, core: 2. Of those that a mesh axis runs over, the one named last changes fastest.
Arguments:
- tokens: bfloat16 [16, 1024, 768], P('dp', 'row', 'col'), may hold values from -6 to 6
- cotangent: bfloat16 [16, 1024, 768], P('dp', 'row', 'col'), may hold values from -6 to 6
- lengths: int32 [16], replicated, may hold values from 256 to 1024, as said below
- assign: int32 [16], replicated, may hold values from 0 to 15, as said below
- norm_gains: float32 [2, 768], P(None, ('col', 'dp')), may hold values from 0.5 to 1.5
- project_weight: float32 [768, 3, 768], P(('col', 'dp'), None, 'row'), may hold values from -0.21875 to 0.21875
- output_weight: float32 [768, 768], P('row', ('col', 'dp')), may hold values from -0.875 to 0.875
- expand_weight: float32 [768, 2, 1152], P(('col', 'dp'), None, 'row'), may hold values from -0.21875 to 0.21875
- shrink_weight: float32 [1152, 768], P('row', ('col', 'dp')), may hold values from -0.1875 to 0.1875
- norm_first: float32 [2, 768], P(None, ('col', 'dp')), may hold values from -64 to 64
- norm_second: float32 [2, 768], P(None, ('col', 'dp')), may hold values from 8.192 to 32.768
- project_first: float32 [768, 3, 768], P(('col', 'dp'), None, 'row'), may hold values from -28 to 28
- project_second: float32 [768, 3, 768], P(('col', 'dp'), None, 'row'), may hold values from 1.6384 to 6.5536
- output_first: float32 [768, 768], P('row', ('col', 'dp')), may hold values from -14 to 14
- output_second: float32 [768, 768], P('row', ('col', 'dp')), may hold values from 0.49152 to 1.96608
- expand_first: float32 [768, 2, 1152], P(('col', 'dp'), None, 'row'), may hold values from -32 to 32
- expand_second: float32 [768, 2, 1152], P(('col', 'dp'), None, 'row'), may hold values from 2.4576 to 9.8304
- shrink_first: float32 [1152, 768], P('row', ('col', 'dp')), may hold values from -40 to 40
- shrink_second: float32 [1152, 768], P('row', ('col', 'dp')), may hold values from 4.096 to 16.384
Outputs:
- mixed: bfloat16 [16, 1024, 768], P('dp', 'row', 'col')
- grad_input: bfloat16 [16, 1024, 768], P('dp', 'row', 'col')
- norm_grad: float32 [2, 768], P(None, ('col', 'dp'))
- norm_mean: float32 [2, 768], P(None, ('col', 'dp'))
- norm_square: float32 [2, 768], P(None, ('col', 'dp'))
- norm_fresh: float32 [2, 768], P(None, ('col', 'dp'))
- project_grad: float32 [768, 3, 768], P(('col', 'dp'), None, 'row')
- project_mean: float32 [768, 3, 768], P(('col', 'dp'), None, 'row')
- project_square: float32 [768, 3, 768], P(('col', 'dp'), None, 'row')
- project_fresh: float32 [768, 3, 768], P(('col', 'dp'), None, 'row')
- output_grad: float32 [768, 768], P('row', ('col', 'dp'))
- output_mean: float32 [768, 768], P('row', ('col', 'dp'))
- output_square: float32 [768, 768], P('row', ('col', 'dp'))
- output_fresh: float32 [768, 768], P('row', ('col', 'dp'))
- expand_grad: float32 [768, 2, 1152], P(('col', 'dp'), None, 'row')
- expand_mean: float32 [768, 2, 1152], P(('col', 'dp'), None, 'row')
- expand_square: float32 [768, 2, 1152], P(('col', 'dp'), None, 'row')
- expand_fresh: float32 [768, 2, 1152], P(('col', 'dp'), None, 'row')
- shrink_grad: float32 [1152, 768], P('row', ('col', 'dp'))
- shrink_mean: float32 [1152, 768], P('row', ('col', 'dp'))
- shrink_square: float32 [1152, 768], P('row', ('col', 'dp'))
- shrink_fresh: float32 [1152, 768], P('row', ('col', 'dp'))
The draws below stay inside these ranges and needn't reach their ends.
Inputs may be any that keep to these rules, and one draw needn't show every extreme that they name: Slot s holds lengths[assign[s]] counted positions; one sequence counts all 1024 positions and another exactly 256. `assign`: A permutation of the sequence numbers.
All inputs are finite; a program needn't handle non-finite values.
Results may differ from the reference program's by a relative error of at most 0.015.
The reference program's roundings to bfloat16 on the way count: a program that leaves them out, or rounds other values in their place, can miss the bound.
Values may be sent and summed in bfloat16 or wider, within the bound.
No kernel may reach another device: no remote copies, remote signals or barrier semaphores. Data moves between devices by JAX's collectives and lax.ppermute only.
A program may use at most 128 MiB of HBM per device.

```python
import math
import jax
import jax.numpy as jnp
from jax import lax

D = 768
HEADS = 12
HEAD = 64
FF = 1152
L = 1024
STEP = 10
SEQS = 16
TOKENS = 16384


def slot_plan(key):
    order = jax.random.permutation(key, SEQS)
    base = jax.random.randint(jax.random.fold_in(key, 1), (SEQS,), L // 4, L + 1)
    longest = jax.random.randint(jax.random.fold_in(key, 2), (), 0, SEQS)
    offset = jax.random.randint(jax.random.fold_in(key, 3), (), 1, SEQS)
    shortest = (longest + offset) % SEQS
    slots = jnp.arange(SEQS, dtype=jnp.int32)
    slot_length = jnp.where(slots == longest, L, base)
    slot_length = jnp.where(slots == shortest, L // 4, slot_length)
    return (order.astype(jnp.int32), slot_length.astype(jnp.int32))


def draw_lengths(key, part):
    order, slot_length = slot_plan(key)
    return jnp.zeros((SEQS,), jnp.int32).at[order].set(slot_length)


def draw_assign(key, part):
    order, slot_length = slot_plan(key)
    return order


def block_levels(key, extent, pieces, low, top_value):
    level, own = 1.0, jax.random.fold_in(key, 6)
    for axis_at, blocks in pieces:
        draws = jnp.exp(jax.random.uniform(jax.random.fold_in(own, axis_at), (blocks,), jnp.float32, low / len(pieces), top_value / len(pieces)))
        level = level * jnp.repeat(draws, extent[axis_at] // blocks).reshape([-1 if axis == axis_at else 1 for axis in range(len(extent))])
    return level


def normal_values(own_key, extent, deviation, bound, shards=(), kind=jnp.bfloat16):
    values = deviation * jax.random.normal(own_key, extent, jnp.float32)
    if shards:
        values = values * block_levels(own_key, extent, shards, -0.22, 0.18)
    return jnp.clip(values, -bound, bound).astype(kind)


def setup_inputs(seed: int = 0) -> dict:
    key_list = jax.random.split(jax.random.key(seed), 20)
    return {
        "tokens": normal_values(key_list[0], (SEQS, L, D), 1.0, 6.0, ((0, 16), (1, 2), (2, 4))),
        "cotangent": normal_values(key_list[1], (SEQS, L, D), 1.0, 6.0, ((0, 16), (1, 2), (2, 4))),
        "lengths": draw_lengths(jax.random.fold_in(key_list[19], 71), 0),
        "assign": draw_assign(jax.random.fold_in(key_list[19], 71), 0),
        "norm_gains": jnp.clip(1.0 + 0.1 * jax.random.normal(key_list[4], (2, D), jnp.float32), 0.5, 1.5),
        "project_weight": normal_values(key_list[5], (D, 3, D), D ** -0.5, 0.21875, ((0, 64), (2, 2)), jnp.float32),
        "output_weight": normal_values(key_list[6], (D, D), (D // 16) ** -0.5, 0.875, ((0, 2), (1, 64)), jnp.float32),
        "expand_weight": normal_values(key_list[7], (D, 2, FF), D ** -0.5, 0.21875, ((0, 64), (2, 2)), jnp.float32),
        "shrink_weight": normal_values(key_list[8], (FF, D), FF ** -0.5, 0.1875, ((0, 2), (1, 64)), jnp.float32),
        "norm_first": normal_values(key_list[9], (2, D), (0.11 * (0.5 * TOKENS) ** 0.5), 64.0, ((1, 64),), jnp.float32),
        "norm_second": jnp.clip(jnp.exp(math.log(32.768) - 1.3862944 * jax.random.uniform(key_list[10], (2, D), jnp.float32) ** block_levels(key_list[10], (2, D), ((1, 64),), -0.2, 0.2)), 8.192, 32.768),
        "project_first": normal_values(key_list[11], (D, 3, D), (0.11 * (0.1 * TOKENS) ** 0.5), 28.0, ((0, 64), (2, 2)), jnp.float32),
        "project_second": jnp.clip(jnp.exp(math.log(6.5536) - 1.3862944 * jax.random.uniform(key_list[12], (D, 3, D), jnp.float32) ** block_levels(key_list[12], (D, 3, D), ((0, 64), (2, 2)), -0.2, 0.2)), 1.6384, 6.5536),
        "output_first": normal_values(key_list[13], (D, D), (0.11 * (0.03 * TOKENS) ** 0.5), 14.0, ((0, 2), (1, 64)), jnp.float32),
        "output_second": jnp.clip(jnp.exp(math.log(1.96608) - 1.3862944 * jax.random.uniform(key_list[14], (D, D), jnp.float32) ** block_levels(key_list[14], (D, D), ((0, 2), (1, 64)), -0.2, 0.2)), 0.49152, 1.96608),
        "expand_first": normal_values(key_list[15], (D, 2, FF), (0.11 * (0.15 * TOKENS) ** 0.5), 32.0, ((0, 64), (2, 2)), jnp.float32),
        "expand_second": jnp.clip(jnp.exp(math.log(9.8304) - 1.3862944 * jax.random.uniform(key_list[16], (D, 2, FF), jnp.float32) ** block_levels(key_list[16], (D, 2, FF), ((0, 64), (2, 2)), -0.2, 0.2)), 2.4576, 9.8304),
        "shrink_first": normal_values(key_list[17], (FF, D), (0.11 * (0.25 * TOKENS) ** 0.5), 40.0, ((0, 2), (1, 64)), jnp.float32),
        "shrink_second": jnp.clip(jnp.exp(math.log(16.384) - 1.3862944 * jax.random.uniform(key_list[18], (FF, D), jnp.float32) ** block_levels(key_list[18], (FF, D), ((0, 2), (1, 64)), -0.2, 0.2)), 4.096, 16.384),
    }


@jax.custom_vjp
def low(v):
    return lax.optimization_barrier(v.astype(jnp.bfloat16)).astype(jnp.float32)

@jax.custom_vjp
def low_back(v):
    return v

def low_keep(v):
    return (low(v), None)

def low_pass(kept, grad):
    return (grad,)

def back_keep(v):
    return (v, None)

def back_low(kept, grad):
    return (low(grad),)
low.defvjp(low_keep, low_pass)
low_back.defvjp(back_keep, back_low)
eps_norm = 1e-05
rope_base = 160000.0
beta_one = 0.9
beta_two = 0.999
adam_eps = 1e-08
rate_matrix = 0.05
rate_gain = 0.3
decay_matrix = 0.01
masked_score = -1e+30
highest = lax.Precision.HIGHEST

def layer_norm(value, gain):
    average = lax.optimization_barrier(jnp.mean(value, axis=-1, keepdims=True))
    spread = lax.optimization_barrier(jnp.mean(value * value, axis=-1, keepdims=True)) - average * average
    return (value - average) * lax.rsqrt(spread + eps_norm) * gain

def rotary(values, positions):
    half = values.shape[-1] // 2
    freqs = rope_base ** (-(2.0 * jnp.arange(half, dtype=jnp.float32)) / values.shape[-1])
    angles = positions.astype(jnp.float32)[:, None] * freqs[None, :]
    cosine = jnp.concatenate([jnp.cos(angles), jnp.cos(angles)], axis=-1)[:, None, :]
    sine = jnp.concatenate([jnp.sin(angles), jnp.sin(angles)], axis=-1)[:, None, :]
    turned = jnp.concatenate([-values[..., half:], values[..., :half]], axis=-1)
    return values * cosine + turned * sine

def gated_gelu(expanded):
    return jax.nn.gelu(expanded[..., 0, :], approximate=False) * expanded[..., 1, :]

def sequence_layer(inputs, length, gains, project, output, expand, shrink):
    count = inputs.shape[0]
    positions = jnp.arange(count, dtype=jnp.int32)
    normed_one = low(layer_norm(inputs, gains[0]))
    projected = low_back(jnp.dot(normed_one, project.reshape(D, 3 * D), precision=highest))
    projected = projected.reshape(count, 3, HEADS, HEAD)
    queries = low(rotary(projected[:, 0], positions))
    keys = low(rotary(projected[:, 1], positions))
    values = low(projected[:, 2])
    raw = low_back(jnp.einsum('qhe,khe->hqk', queries, keys, precision=highest))
    keep = (positions < length)[None, None, :]
    score = jnp.where(keep, raw * HEAD ** (-0.5), masked_score)
    log_total = jax.nn.logsumexp(score, axis=-1, keepdims=True)
    probs = low(jnp.exp(score - log_total))
    attended = low_back(low(jnp.einsum('hqk,khe->qhe', probs, values, precision=highest)))
    attended = attended.reshape(count, D)
    mid = inputs + low_back(jnp.dot(attended, output, precision=highest))
    normed_two = low(layer_norm(mid, gains[1]))
    expanded = low_back(jnp.dot(normed_two, expand.reshape(D, 2 * FF), precision=highest))
    hidden = low(gated_gelu(expanded.reshape(count, 2, FF)))
    return mid + low_back(jnp.dot(hidden, shrink, precision=highest))

def adam_update(param, grad, first, second, rate, decay):
    first_new = beta_one * first + (1.0 - beta_one) * grad
    second_new = beta_two * second + (1.0 - beta_two) * grad * grad
    mean_hat = first_new / (1.0 - beta_one ** STEP)
    square_hat = second_new / (1.0 - beta_two ** STEP)
    fresh = param - rate * (mean_hat / (jnp.sqrt(square_hat) + adam_eps) + decay * param)
    return (grad, first_new, second_new, fresh)

def reference(tokens, cotangent, lengths, assign, norm_gains, project_weight, output_weight, expand_weight, shrink_weight, norm_first, norm_second, project_first, project_second, output_first, output_second, expand_first, expand_second, shrink_first, shrink_second):
    slot_length = lengths[assign].astype(jnp.int32)

    def forward(inputs, gains, project, output, expand, shrink):
        gains_low = low(gains)
        project_low = low(project)
        output_low = low(output)
        expand_low = low(expand)
        shrink_low = low(shrink)

        def one_slot(pair):
            return sequence_layer(pair[0], pair[1], gains_low, project_low, output_low, expand_low, shrink_low)
        return lax.map(jax.checkpoint(one_slot), (inputs, slot_length))
    inputs = tokens.astype(jnp.float32)
    result, pull = jax.vjp(forward, inputs, norm_gains, project_weight, output_weight, expand_weight, shrink_weight)
    counted = (jnp.arange(L, dtype=jnp.int32)[None, :] < slot_length[:, None])[:, :, None]
    back = jnp.where(counted, cotangent.astype(jnp.float32), jnp.zeros_like(inputs))
    grads = pull(back)
    mixed = result.astype(jnp.bfloat16)
    grad_input = grads[0].astype(jnp.bfloat16)
    norm_part = adam_update(norm_gains, grads[1], norm_first, norm_second, rate_gain, 0.0)
    project_part = adam_update(project_weight, grads[2], project_first, project_second, rate_matrix, decay_matrix)
    output_part = adam_update(output_weight, grads[3], output_first, output_second, rate_matrix, decay_matrix)
    expand_part = adam_update(expand_weight, grads[4], expand_first, expand_second, rate_matrix, decay_matrix)
    shrink_part = adam_update(shrink_weight, grads[5], shrink_first, shrink_second, rate_matrix, decay_matrix)
    return (mixed, grad_input, norm_part[0], norm_part[1], norm_part[2], norm_part[3], project_part[0], project_part[1], project_part[2], project_part[3], output_part[0], output_part[1], output_part[2], output_part[3], expand_part[0], expand_part[1], expand_part[2], expand_part[3], shrink_part[0], shrink_part[1], shrink_part[2], shrink_part[3])
```

```python
import itertools

import jax
import jax.numpy as jnp
import numpy as np
from jax import lax
from jax.sharding import Mesh, PartitionSpec as P

HEAD = 64
STEP = 10


eps_norm = 1e-05
rope_base = 160000.0
beta_one = 0.9
beta_two = 0.999
adam_eps = 1e-08
rate_matrix = 0.05
rate_gain = 0.3
decay_matrix = 0.01
masked_score = -1e30

SIZES = {"xh": 2, "z": 4, "core": 2, "row": 2, "col": 4}
LANE = 128
BF16 = jnp.bfloat16
F32 = jnp.float32


def move(value, axes, target):
    sizes = [SIZES[axis] for axis in axes]

    def flat(place):
        return int(np.ravel_multi_index(place, sizes))

    pairs = [
        (flat(place), flat(target(*place))) for place in itertools.product(*map(range, sizes))
    ]
    return lax.ppermute(value, axes, pairs)


def swap_cores(value):
    return move(value, ("core",), lambda core: (core ^ 1,))


def sum_cores(partial_value):
    return partial_value + swap_cores(partial_value)


def ordered(flag, first, second):
    return jnp.where(flag == 0, first, second), jnp.where(flag == 0, second, first)


def pick(array, index):
    return lax.dynamic_index_in_dim(array, index, 0, keepdims=False)


def owner_move(value, flip):
    return move(
        value,
        ("xh", "core", "row"),
        lambda xh, core, row: (xh ^ (flip >> 1), row, core ^ (flip & 1)),
    )


def owner_return(value, flip):
    return move(
        value,
        ("xh", "core", "row"),
        lambda xh, core, row: (xh ^ (flip >> 1), row ^ (flip & 1), core),
    )


def shift(value, axis, step):
    return move(value, (axis,), lambda place: ((place + step) % SIZES[axis],))


def gather_x(shard):
    own = [owner_move(shard, flip) for flip in range(4)]
    row, xh = lax.axis_index("row"), lax.axis_index("xh")
    near = jnp.concatenate(ordered(row, own[0], own[1]), axis=0)
    far = jnp.concatenate(ordered(row, own[2], own[3]), axis=0)
    return jnp.concatenate(ordered(xh, near, far), axis=0)


def gather_ring(block, axis):
    here = lax.axis_index(axis)
    pieces = [block] + [shift(block, axis, step) for step in (1, 2, 3)]
    out = jnp.zeros((4,) + block.shape, block.dtype)
    for step, piece in enumerate(pieces):
        out = lax.dynamic_update_index_in_dim(out, piece, (here - step) % 4, 0)
    return out


def gather_weights(shard):
    width = shard.shape[1]
    block = gather_x(shard)
    part = block.shape[0] // 2
    block = gather_ring(block, "z").reshape(4, 2, part, width)
    block = jnp.swapaxes(block, 0, 1).reshape(8 * part, width)
    return gather_ring(block, "col").reshape(-1, width)


def scatter_ring(blocks, axis):
    here = lax.axis_index(axis)
    total = pick(blocks, here)
    for step in (1, 2, 3):
        total = total + shift(pick(blocks, (here + step) % 4).astype(BF16), axis, step).astype(F32)
    return total


def scatter_grads(grad):
    rows, width = grad.shape
    block = scatter_ring(grad.reshape(4, rows // 4, width), "col")
    part = rows // 32
    block = jnp.swapaxes(block.reshape(2, 4, part, width), 0, 1)
    block = scatter_ring(block, "z").astype(BF16)
    row, xh = lax.axis_index("row"), lax.axis_index("xh")
    near, far = ordered(xh, block[0], block[1])
    pieces = ordered(row, near[: part // 2], near[part // 2 :]) + ordered(
        row, far[: part // 2], far[part // 2 :]
    )
    return sum(owner_return(piece, flip).astype(F32) for flip, piece in enumerate(pieces))


def chip_move(value, flip):
    return move(
        value, ("core", "col"), lambda core, col: (col >> 1, 2 * core + ((col & 1) ^ flip))
    )


def to_chip(value):
    core, odd = lax.axis_index("core"), lax.axis_index("col") & 1
    rows = value.shape[0] // 2
    halves = ordered(odd, value[:rows], value[rows:])
    received = [chip_move(half, flip) for flip, half in enumerate(halves)]
    mine = jnp.concatenate(ordered(odd, *received), axis=1)
    return jnp.concatenate(ordered(core, mine, swap_cores(mine)), axis=1)


def from_chip(value):
    core, odd = lax.axis_index("core"), lax.axis_index("col") & 1
    half = value.shape[1] // 2
    mine = jnp.where(core == 0, value[:, :half], value[:, half:])
    pieces = ordered(odd, mine[:, : half // 2], mine[:, half // 2 :])
    received = [chip_move(piece, flip) for flip, piece in enumerate(pieces)]
    return jnp.concatenate(ordered(odd, *received), axis=0)


SQUARE = ((1, 0), (0, 1), (1, 1))


def square_move(value, flip_row, flip_col):
    return move(value, ("row", "col"), lambda row, col: (row ^ flip_row, col ^ flip_col))


def rotary_tables(positions):
    half = HEAD // 2
    freqs = rope_base ** (-(2.0 * jnp.arange(half, dtype=F32)) / HEAD)
    angles = positions.astype(F32)[:, None] * freqs[None, :]
    cosine = jnp.concatenate([jnp.cos(angles), jnp.cos(angles)], axis=-1)[:, None, :]
    sine = jnp.concatenate([jnp.sin(angles), jnp.sin(angles)], axis=-1)[:, None, :]
    return cosine, sine


def rotary(values, tables):
    half = HEAD // 2
    turned = jnp.concatenate([-values[..., half:], values[..., :half]], axis=-1)
    return values * tables[0] + turned * tables[1]


def unrotary(grads, tables):
    half = HEAD // 2
    turned = grads * tables[1]
    return grads * tables[0] + jnp.concatenate([turned[..., half:], -turned[..., :half]], axis=-1)


def gated_gelu(expanded):
    return jax.nn.gelu(expanded[..., 0, :], approximate=False) * expanded[..., 1, :]


def product(left, right):
    return lax.dot_general(left, right, (((1,), (0,)), ((), ())), preferred_element_type=F32)


def product_turned(left, right):
    return lax.dot_general(left, right, (((1,), (1,)), ((), ())), preferred_element_type=F32)


def token_product(left, right):
    return lax.dot_general(left, right, (((0,), (0,)), ((), ())), preferred_element_type=F32)


def norm_forward(value):
    count = value.shape[-1]
    average = jnp.sum(value, axis=-1, keepdims=True) / count
    spread = jnp.sum(value * value, axis=-1, keepdims=True) / count - average * average
    inverse = lax.rsqrt(spread + eps_norm)
    return ((value - average) * inverse, inverse)


def norm_backward(grad_out, centered, inverse, gain):
    count = grad_out.shape[-1]
    scaled = grad_out * gain
    total = jnp.sum(scaled, axis=-1, keepdims=True)
    along = jnp.sum(scaled * centered, axis=-1, keepdims=True)
    grad_value = inverse * (scaled - total / count - centered * (along / count))
    grad_gain = jnp.sum(grad_out * centered, axis=0)
    return (grad_value, grad_gain)


def adam_update(param, grad, first, second, rate, decay):
    first_new = beta_one * first + (1.0 - beta_one) * grad
    second_new = beta_two * second + (1.0 - beta_two) * grad * grad
    mean_hat = first_new / (1.0 - beta_one**STEP)
    square_hat = second_new / (1.0 - beta_two**STEP)
    fresh = param - rate * (mean_hat / (jnp.sqrt(square_hat) + adam_eps) + decay * param)
    return (grad, first_new, second_new, fresh)


def scores_of(queries, keys, keep):
    raw = jnp.einsum("qhe,khe->hqk", queries, keys, preferred_element_type=F32)
    return jnp.where(keep, raw * HEAD ** (-0.5), masked_score)


def attention_forward(queries, keys, values, keep):
    scores = scores_of(queries, keys, keep)
    log_total = jax.nn.logsumexp(scores, axis=-1, keepdims=True)
    probs_low = jnp.exp(scores - log_total).astype(BF16)
    attended = jnp.einsum("hqk,khe->qhe", probs_low, values, preferred_element_type=F32)
    return attended.astype(BF16), log_total


def attention_backward(queries, keys, values, keep, log_total, grad_attended):
    probs = jnp.exp(scores_of(queries, keys, keep) - log_total)
    grad_probs = jnp.einsum("qhe,khe->hqk", grad_attended, values, preferred_element_type=F32)
    centre = jnp.sum(probs * grad_probs, axis=-1, keepdims=True)
    grad_raw = (probs * (grad_probs - centre) * HEAD ** (-0.5)).astype(BF16)
    grad_queries = jnp.einsum("hqk,khe->qhe", grad_raw, keys, preferred_element_type=F32)
    grad_keys = jnp.einsum("hqk,qhe->khe", grad_raw, queries, preferred_element_type=F32)
    grad_values = jnp.einsum(
        "hqk,qhe->khe", probs.astype(BF16), grad_attended, preferred_element_type=F32
    )
    return grad_queries, grad_keys, grad_values


def on_device(
    tokens,
    cotangent,
    lengths,
    assign,
    norm_gains,
    project_weight,
    output_weight,
    expand_weight,
    shrink_weight,
    norm_first,
    norm_second,
    project_first,
    project_second,
    output_first,
    output_second,
    expand_first,
    expand_second,
    shrink_first,
    shrink_second,
):
    row, col = lax.axis_index("row"), lax.axis_index("col")
    shard_rows = project_weight.shape[0]
    project_width = 3 * project_weight.shape[2]
    output_width = output_weight.shape[0]
    expand_width = 2 * expand_weight.shape[2]
    shrink_width = shrink_weight.shape[0]
    heads_here = output_width // HEAD

    slot = (lax.axis_index("xh") * 4 + lax.axis_index("z")) * 2 + (col >> 1)
    catalog = jnp.arange(lengths.shape[0], dtype=jnp.int32)
    seq_id = jnp.sum(jnp.where(catalog == slot, assign, 0))
    slot_length = jnp.sum(jnp.where(catalog == seq_id, lengths, 0))
    block_rows = tokens.shape[1] // 2
    within = jnp.arange(block_rows, dtype=jnp.int32)

    def block_positions(flip_row, flip_col):
        return (2 * (row ^ flip_row) + ((col & 1) ^ flip_col)) * block_rows + within

    positions = block_positions(0, 0)
    key_pos = jnp.concatenate([positions] + [block_positions(*flips) for flips in SQUARE])
    keep = (key_pos < slot_length)[None, None, :]

    pad = -(-2 // LANE) * LANE
    first_shard = jnp.concatenate(
        [
            project_weight.reshape(shard_rows, project_width),
            norm_gains.T,
            jnp.zeros((shard_rows, pad - 2), F32),
        ],
        axis=1,
    ).astype(BF16)
    rest_width = output_width + expand_width + shrink_width
    rest_pad = -rest_width % LANE
    rest_shard = jnp.concatenate(
        [
            output_weight.T,
            expand_weight.reshape(shard_rows, expand_width),
            shrink_weight.T,
            jnp.zeros((shard_rows, rest_pad), F32),
        ],
        axis=1,
    ).astype(BF16)
    first_all = gather_weights(first_shard)
    inputs = to_chip(tokens[0]).astype(F32)
    rest_all = gather_weights(rest_shard)
    cotangent_chip = to_chip(cotangent[0])
    back = jnp.where(
        (positions < slot_length)[:, None], cotangent_chip, jnp.zeros_like(cotangent_chip)
    )
    project_low = first_all[:, :project_width]
    gains_low = first_all[:, project_width : project_width + 2].astype(F32)
    gain_one, gain_two = gains_low[:, 0], gains_low[:, 1]
    output_turned = rest_all[:, :output_width]
    expand_low = rest_all[:, output_width : output_width + expand_width]
    shrink_turned = rest_all[:, output_width + expand_width : rest_width]

    centered_one, inverse_one = norm_forward(inputs)
    normed_one = (centered_one * gain_one).astype(BF16)
    projected = product(normed_one, project_low).reshape(block_rows, 3, heads_here, HEAD)
    tables = rotary_tables(positions)
    queries = rotary(projected[:, 0], tables).astype(BF16)
    keys_own = rotary(projected[:, 1], tables).astype(BF16)
    values_own = projected[:, 2].astype(BF16)
    own = jnp.concatenate(
        [keys_own.reshape(block_rows, -1), values_own.reshape(block_rows, -1)], axis=1
    )
    pairs = jnp.concatenate([own] + [square_move(own, *flips) for flips in SQUARE], axis=0)
    keys = pairs[:, :output_width].reshape(-1, heads_here, HEAD)
    values = pairs[:, output_width:].reshape(-1, heads_here, HEAD)

    attended, log_total = attention_forward(queries, keys, values, keep)
    attended = attended.reshape(block_rows, -1)
    middle = inputs + sum_cores(product_turned(attended, output_turned))
    centered_two, inverse_two = norm_forward(middle)
    normed_two = (centered_two * gain_two).astype(BF16)
    expanded = product(normed_two, expand_low).reshape(block_rows, 2, -1)
    hidden = gated_gelu(expanded).astype(BF16)
    mixed = (middle + sum_cores(product_turned(hidden, shrink_turned))).astype(BF16)
    mixed_home = from_chip(mixed)

    grad_hidden = product(back, shrink_turned)
    grad_expanded = jax.vjp(gated_gelu, expanded)[1](grad_hidden)[0].astype(BF16)
    grad_expanded = grad_expanded.reshape(block_rows, -1)
    grad_normed_two = sum_cores(product_turned(grad_expanded, expand_low))
    grad_mid_norm, gain_grad_two = norm_backward(
        grad_normed_two, centered_two, inverse_two, gain_two
    )
    grad_mid = back.astype(F32) + grad_mid_norm
    grad_mid_low = grad_mid.astype(BF16)
    grad_attended = product(grad_mid_low, output_turned).astype(BF16)
    rest_grad = jnp.concatenate(
        [
            token_product(grad_mid_low, attended),
            token_product(normed_two, grad_expanded),
            token_product(back, hidden),
            gain_grad_two[:, None],
            jnp.zeros((middle.shape[1], rest_pad - 1), F32),
        ],
        axis=1,
    )
    rest_owned = scatter_grads(rest_grad)

    grad_queries, key_parts, value_parts = attention_backward(
        queries, keys, values, keep, log_total, grad_attended.reshape(block_rows, heads_here, HEAD)
    )
    parts = jnp.concatenate(
        [key_parts.reshape(-1, output_width), value_parts.reshape(-1, output_width)], axis=1
    ).reshape(4, block_rows, 2 * output_width)
    pair_grad = parts[0]
    for index, flips in enumerate(SQUARE):
        pair_grad = pair_grad + square_move(parts[index + 1].astype(BF16), *flips).astype(F32)
    grad_keys = pair_grad[:, :output_width].reshape(block_rows, heads_here, HEAD)
    grad_projected = jnp.concatenate(
        [
            unrotary(grad_queries, tables).reshape(block_rows, -1),
            unrotary(grad_keys, tables).reshape(block_rows, -1),
            pair_grad[:, output_width:],
        ],
        axis=1,
    ).astype(BF16)
    grad_normed_one = sum_cores(product_turned(grad_projected, project_low))
    grad_input_norm, gain_grad_one = norm_backward(
        grad_normed_one, centered_one, inverse_one, gain_one
    )
    grad_input = from_chip((grad_mid + grad_input_norm).astype(BF16))
    first_grad = jnp.concatenate(
        [
            token_product(normed_one, grad_projected),
            gain_grad_one[:, None],
            jnp.zeros((middle.shape[1], pad - 1), F32),
        ],
        axis=1,
    )
    first_owned = scatter_grads(first_grad)

    project_grad = first_owned[:, :project_width].reshape(project_weight.shape)
    output_grad = rest_owned[:, :output_width].T
    expand_grad = rest_owned[:, output_width : output_width + expand_width].reshape(
        expand_weight.shape
    )
    shrink_grad = rest_owned[:, output_width + expand_width : rest_width].T
    gain_grad = jnp.stack([first_owned[:, project_width], rest_owned[:, rest_width]])
    return (
        (mixed_home[None], grad_input[None])
        + adam_update(norm_gains, gain_grad, norm_first, norm_second, rate_gain, 0.0)
        + adam_update(
            project_weight, project_grad, project_first, project_second, rate_matrix, decay_matrix
        )
        + adam_update(
            output_weight, output_grad, output_first, output_second, rate_matrix, decay_matrix
        )
        + adam_update(
            expand_weight, expand_grad, expand_first, expand_second, rate_matrix, decay_matrix
        )
        + adam_update(
            shrink_weight, shrink_grad, shrink_first, shrink_second, rate_matrix, decay_matrix
        )
    )


def solution(mesh):
    fine = Mesh(mesh.devices.reshape(tuple(SIZES.values())), tuple(SIZES))
    dp = ("xh", "z", "core")
    owners = ("col",) + dp
    active = P(dp, "row", "col")
    gains = P(None, owners)
    features_first = P(owners, None, "row")
    features_last = P("row", owners)
    params = (gains, features_first, features_last, features_first, features_last)
    moments = tuple(spec for spec in params for _ in range(2))
    results = tuple(spec for spec in params for _ in range(4))
    return jax.shard_map(
        on_device,
        mesh=fine,
        in_specs=(active, active, P(), P()) + params + moments,
        out_specs=(active, active) + results,
        check_vma=False,
    )
```

```python
import itertools

import jax
import jax.numpy as jnp
import numpy as np
from jax import lax
from jax.experimental import pallas as pl
from jax.experimental.pallas import tpu as pltpu
from jax.sharding import Mesh, PartitionSpec as P

HEAD = 64
STEP = 10


eps_norm = 1e-05
rope_base = 160000.0
beta_one = 0.9
beta_two = 0.999
adam_eps = 1e-08
rate_matrix = 0.05
rate_gain = 0.3
decay_matrix = 0.01
masked_score = -1e30

SIZES = {"xh": 2, "z": 4, "core": 2, "row": 2, "col": 4}
LANE = 128
BF16 = jnp.bfloat16
F32 = jnp.float32


def move(value, axes, target):
    sizes = [SIZES[axis] for axis in axes]

    def flat(place):
        return int(np.ravel_multi_index(place, sizes))

    pairs = [
        (flat(place), flat(target(*place))) for place in itertools.product(*map(range, sizes))
    ]
    return lax.ppermute(value, axes, pairs)


def swap_cores(value):
    return move(value, ("core",), lambda core: (core ^ 1,))


def sum_cores(partial_value):
    return partial_value + swap_cores(partial_value)


def ordered(flag, first, second):
    return jnp.where(flag == 0, first, second), jnp.where(flag == 0, second, first)


def owner_move(value, flip):
    return move(
        value,
        ("xh", "core", "row"),
        lambda xh, core, row: (xh ^ (flip >> 1), row, core ^ (flip & 1)),
    )


def owner_return(value, flip):
    return move(
        value,
        ("xh", "core", "row"),
        lambda xh, core, row: (xh ^ (flip >> 1), row ^ (flip & 1), core),
    )


def shift(value, axis, step):
    return move(value, (axis,), lambda place: ((place + step) % SIZES[axis],))


def gather_x(shard):
    own = [owner_move(shard, flip) for flip in range(4)]
    row, xh = lax.axis_index("row"), lax.axis_index("xh")
    near = jnp.concatenate(ordered(row, own[0], own[1]), axis=0)
    far = jnp.concatenate(ordered(row, own[2], own[3]), axis=0)
    return jnp.concatenate(ordered(xh, near, far), axis=0)


def gather_ring(block, axis):
    here = lax.axis_index(axis)
    pieces = [block] + [shift(block, axis, step) for step in (1, 2, 3)]
    out = jnp.zeros((4,) + block.shape, block.dtype)
    for step, piece in enumerate(pieces):
        out = lax.dynamic_update_index_in_dim(out, piece, (here - step) % 4, 0)
    return out


def by_z_first(block):
    width = block.shape[-1]
    return jnp.swapaxes(block.reshape(4, 2, -1, width), 0, 1).reshape(-1, width)


def by_z_last(block):
    width = block.shape[-1]
    return jnp.swapaxes(block.reshape(4, 8, -1, width), 0, 1).reshape(-1, width)


def ring_pieces(block, axis):
    return [block] + [shift(block, axis, step) for step in (1, 2, 3)]


def scatter_ring(blocks, axis, dim=0):
    here = lax.axis_index(axis)

    def pick_at(index):
        return lax.dynamic_index_in_dim(blocks, index, dim, keepdims=False)

    total = pick_at(here).astype(F32)
    for step in (1, 2, 3):
        total = total + shift(pick_at((here + step) % 4), axis, step).astype(F32)
    return total


def scatter_col(grad):
    rows, width = grad.shape
    return scatter_ring(grad.reshape(4, rows // 4, width), "col")


def exchange_sum(blocks, axis):
    received = lax.all_to_all(blocks, axis, split_axis=0, concat_axis=0)
    return jnp.sum(received.astype(F32), axis=0).astype(BF16)


def scatter_x(block):
    rows = block.shape[0] // 4
    row, xh = lax.axis_index("row"), lax.axis_index("xh")
    near, far = ordered(xh, block[: 2 * rows], block[2 * rows :])
    pieces = ordered(row, near[:rows], near[rows:]) + ordered(row, far[:rows], far[rows:])
    return sum(owner_return(piece, flip).astype(F32) for flip, piece in enumerate(pieces))


def chip_move(value, flip):
    return move(
        value, ("core", "col"), lambda core, col: (col >> 1, 2 * core + ((col & 1) ^ flip))
    )


def to_chip(value):
    odd = lax.axis_index("col") & 1
    rows = value.shape[0] // 2
    halves = ordered(odd, value[:rows], value[rows:])
    return ordered(odd, *[chip_move(half, flip) for flip, half in enumerate(halves)])


def join_cores(value):
    return jnp.concatenate(ordered(lax.axis_index("core"), value, swap_cores(value)), axis=1)


def from_chip(value):
    core, odd = lax.axis_index("core"), lax.axis_index("col") & 1
    half = value.shape[1] // 2
    mine = jnp.where(core == 0, value[:, :half], value[:, half:])
    pieces = ordered(odd, mine[:, : half // 2], mine[:, half // 2 :])
    received = [chip_move(piece, flip) for flip, piece in enumerate(pieces)]
    return jnp.concatenate(ordered(odd, *received), axis=0)


SQUARE = ((1, 0), (0, 1), (1, 1))


def square_move(value, flip_row, flip_col):
    return move(value, ("row", "col"), lambda row, col: (row ^ flip_row, col ^ flip_col))


def rotary_tables(positions):
    half = HEAD // 2
    freqs = rope_base ** (-(2.0 * jnp.arange(half, dtype=F32)) / HEAD)
    angles = positions.astype(F32)[:, None] * freqs[None, :]
    cosine, sine = jnp.cos(angles), jnp.sin(angles)
    return (
        jnp.concatenate([cosine] * 4, axis=-1),
        jnp.concatenate([-sine, sine, -sine, sine], axis=-1),
    )


def turned(values):
    lane = lax.broadcasted_iota(jnp.int32, values.shape, 1)
    first = lane % HEAD < HEAD // 2
    back, ahead = pltpu.roll(values, LANE - HEAD // 2, 1), pltpu.roll(values, HEAD // 2, 1)
    return jnp.where(first, back, ahead)


def product(left, right):
    return lax.dot_general(left, right, (((1,), (0,)), ((), ())), preferred_element_type=F32)


def product_turned(left, right):
    return lax.dot_general(left, right, (((1,), (1,)), ((), ())), preferred_element_type=F32)


def token_product(left, right):
    return lax.dot_general(left, right, (((0,), (0,)), ((), ())), preferred_element_type=F32)


def norm_forward(value):
    count = value.shape[-1]
    average = jnp.sum(value, axis=-1, keepdims=True) / count
    spread = jnp.sum(value * value, axis=-1, keepdims=True) / count - average * average
    inverse = lax.rsqrt(spread + eps_norm)
    return ((value - average) * inverse, inverse)


def norm_backward(grad_out, centered, inverse, gain):
    count = grad_out.shape[-1]
    scaled = grad_out * gain
    total = jnp.sum(scaled, axis=-1, keepdims=True)
    along = jnp.sum(scaled * centered, axis=-1, keepdims=True)
    grad_value = inverse * (scaled - total / count - centered * (along / count))
    grad_gain = jnp.sum(grad_out * centered, axis=0)
    return (grad_value, grad_gain)


def adam_update(param, grad, first, second, rate, decay):
    first_new = beta_one * first + (1.0 - beta_one) * grad
    second_new = beta_two * second + (1.0 - beta_two) * grad * grad
    mean_hat = first_new / (1.0 - beta_one**STEP)
    square_hat = second_new / (1.0 - beta_two**STEP)
    fresh = param - rate * (mean_hat / (jnp.sqrt(square_hat) + adam_eps) + decay * param)
    return (grad, first_new, second_new, fresh)


def kernel_dot(left, right, left_dim, right_dim):
    return lax.dot_general(
        left, right, (((left_dim,), (right_dim,)), ((), ())), preferred_element_type=F32
    )


def kernel_call(body, shapes, *operands, scalars=0):
    return pl.pallas_call(
        body,
        out_shape=tuple(jax.ShapeDtypeStruct(*shape) for shape in shapes),
        in_specs=[pl.BlockSpec(memory_space=pltpu.SMEM)] * scalars
        + [pl.BlockSpec(memory_space=pltpu.VMEM)] * (len(operands) - scalars),
        compiler_params=pltpu.CompilerParams(vmem_limit_bytes=44 * 2**20),
    )(*operands)


def softmax_turned(keep, key, query):
    scores = jnp.where(keep, kernel_dot(key, query, 1, 1) * HEAD ** (-0.5), masked_score)
    exps = jnp.exp(scores - jnp.max(scores, axis=0, keepdims=True))
    return exps * (1.0 / jnp.sum(exps, axis=0, keepdims=True))


def forward_kernel(
    col_ref,
    piece_zero,
    piece_one,
    piece_two,
    piece_three,
    keep_ref,
    centered_ref,
    gain_ref,
    cosine_ref,
    sine_ref,
    weight_out,
    normed_out,
    query_out,
    pair_out,
    attended_out,
):
    width = query_out.shape[1]
    rows = query_out.shape[0]
    col = col_ref[0]
    for step, piece in enumerate((piece_zero, piece_one, piece_two, piece_three)):
        weight_out[(col - step) & 3] = piece[...]
    weight = weight_out[...].reshape(-1, weight_out.shape[2])
    normed_out[...] = (centered_ref[...] * gain_ref[...]).astype(BF16)
    normed = normed_out[...]
    query_at, value_at = width + LANE, 2 * width + LANE

    def rotated(values, count):
        return (values * cosine_ref[:count] + turned(values) * sine_ref[:count]).astype(BF16)

    for start in range(0, width, LANE):
        at = slice(start, start + LANE)
        pair_out[:, at] = rotated(kernel_dot(normed, weight[:, at], 1, 0), normed.shape[0])
        query_out[:, at] = rotated(
            kernel_dot(normed[:rows], weight[:, query_at + start : query_at + start + LANE], 1, 0),
            rows,
        )
    pair_out[:, width:] = kernel_dot(normed, weight[:, value_at : value_at + width], 1, 0).astype(
        BF16
    )
    keep = keep_ref[...] > 0
    for head in range(width // HEAD):
        at = slice(HEAD * head, HEAD * (head + 1))
        values = pair_out[:, width + HEAD * head : width + HEAD * (head + 1)]
        probs_low = softmax_turned(keep, pair_out[:, at], query_out[:, at]).astype(BF16)
        attended_out[:, at] = kernel_dot(probs_low, values, 0, 0).astype(BF16)


def output_kernel(attended_ref, gathered_ref, weight_out, part_out):
    part = gathered_ref.shape[2]
    for group in range(4 * gathered_ref.shape[1]):
        weight_out[group * part : (group + 1) * part] = gathered_ref[group % 4, group // 4]
    width = attended_ref.shape[1]
    part_out[...] = kernel_dot(attended_ref[...], weight_out[:, :width], 1, 1)


def feed_kernel(
    input_ref,
    part_ref,
    other_ref,
    gain_ref,
    weight_ref,
    shrink_ref,
    back_ref,
    centered_out,
    inverse_out,
    normed_out,
    hidden_out,
    grad_out,
    mixed_out,
    normed_grad_out,
):
    units = hidden_out.shape[1]
    middle = input_ref[...].astype(F32) + (part_ref[...] + other_ref[...])
    centered, inverse = norm_forward(middle)
    centered_out[...] = centered
    inverse_out[...] = inverse
    normed = (centered * gain_ref[...]).astype(BF16)
    normed_out[...] = normed
    expand = weight_ref[:, weight_ref.shape[1] - 2 * units :]
    shrink = shrink_ref[:, :units]
    expanded = kernel_dot(normed, expand, 1, 0)
    active, gate = expanded[:, :units], expanded[:, units:]
    phi = 0.5 * (1.0 + lax.erf(active * 0.5**0.5))
    density = jnp.exp(-0.5 * active * active) * (2.0 * np.pi) ** (-0.5)
    gelu = active * phi
    hidden = (gelu * gate).astype(BF16)
    hidden_out[...] = hidden
    mixed_out[...] = 0.5 * middle + kernel_dot(hidden, shrink, 1, 1)
    grad_hidden = kernel_dot(back_ref[...], shrink, 1, 0)
    grad_out[:, :units] = (grad_hidden * gate * (phi + active * density)).astype(BF16)
    grad_out[:, units:] = (grad_hidden * gelu).astype(BF16)
    normed_grad_out[...] = kernel_dot(grad_out[...], expand, 1, 1)


def rest_grads_kernel(normed_ref, grad_ref, back_ref, hidden_ref, out_ref):
    groups, part = out_ref.shape[0] * out_ref.shape[1], out_ref.shape[2]

    def store(result, start):
        for group in range(groups):
            out_ref[group % 4, group // 4, :, start : start + result.shape[1]] = result[
                group * part : (group + 1) * part
            ]

    expand_width, units = grad_ref.shape[1], hidden_ref.shape[1]
    store(kernel_dot(normed_ref[...], grad_ref[...], 0, 0).astype(BF16), 0)
    store(kernel_dot(back_ref[...], hidden_ref[...], 0, 0).astype(BF16), expand_width)
    pad = out_ref.shape[3] - expand_width - units
    store(jnp.zeros((groups * part, pad), BF16), expand_width + units)


def backward_kernel(
    keep_ref,
    part_ref,
    other_ref,
    centered_ref,
    inverse_ref,
    gain_ref,
    back_ref,
    weight_ref,
    query_ref,
    pair_ref,
    normed_ref,
    attended_ref,
    cosine_ref,
    sine_ref,
    middle_out,
    query_out,
    pair_out,
    grads_out,
    query_grad,
    key_grad,
):
    width = query_ref.shape[1]
    rows = query_ref.shape[0]
    grad_norm, _ = norm_backward(
        part_ref[...] + other_ref[...], centered_ref[...], inverse_ref[...], gain_ref[...]
    )
    grad_middle = back_ref[...].astype(F32) + grad_norm
    middle_out[...] = grad_middle
    middle_low = grad_middle.astype(BF16)
    grad_attended = kernel_dot(middle_low, weight_ref[:, :width], 1, 0).astype(BF16)
    keep = keep_ref[...] > 0
    for head in range(width // HEAD):
        at = slice(HEAD * head, HEAD * (head + 1))
        value_at = slice(width + HEAD * head, width + HEAD * (head + 1))
        query, grad = query_ref[:, at], grad_attended[:, at]
        key, value = pair_ref[:, at], pair_ref[:, value_at]
        probs = softmax_turned(keep, key, query)
        grad_probs = kernel_dot(value, grad, 1, 1)
        centre = jnp.sum(probs * grad_probs, axis=0, keepdims=True)
        grad_raw = (probs * (grad_probs - centre) * HEAD ** (-0.5)).astype(BF16)
        query_grad[:, at] = kernel_dot(grad_raw, key, 0, 0)
        key_grad[:, at] = kernel_dot(grad_raw, query, 1, 0)
        pair_out[:, value_at] = kernel_dot(probs.astype(BF16), grad, 1, 0).astype(BF16)

    def unrotated(values, count):
        return (values * cosine_ref[:count] - turned(values) * sine_ref[:count]).astype(BF16)

    for start in range(0, width, LANE):
        at = slice(start, start + LANE)
        query_out[:, at] = unrotated(query_grad[:, at], rows)
        pair_out[:, at] = unrotated(key_grad[:, at], key_grad.shape[0])
    normed = normed_ref[...]
    pair_grads = kernel_dot(normed, pair_out[...], 0, 0).astype(BF16)
    grads_out[:, :width] = pair_grads[:, :width]
    grads_out[:, width : 2 * width] = kernel_dot(normed[:rows], query_out[...], 0, 0).astype(BF16)
    grads_out[:, 2 * width : 3 * width] = pair_grads[:, width:]
    grads_out[:, 3 * width :] = kernel_dot(middle_low, attended_ref[...], 0, 0).astype(BF16)


def on_device(
    tokens,
    cotangent,
    lengths,
    assign,
    norm_gains,
    project_weight,
    output_weight,
    expand_weight,
    shrink_weight,
    norm_first,
    norm_second,
    project_first,
    project_second,
    output_first,
    output_second,
    expand_first,
    expand_second,
    shrink_first,
    shrink_second,
):
    row, col = lax.axis_index("row"), lax.axis_index("col")
    shard_rows = project_weight.shape[0]
    output_width = output_weight.shape[0]
    expand_width = 2 * expand_weight.shape[2]
    shrink_width = shrink_weight.shape[0]
    heads_here = output_width // HEAD

    slot = (lax.axis_index("xh") * 4 + lax.axis_index("z")) * 2 + (col >> 1)
    catalog = jnp.arange(lengths.shape[0], dtype=jnp.int32)
    seq_id = jnp.sum(jnp.where(catalog == slot, assign, 0))
    slot_length = jnp.sum(jnp.where(catalog == seq_id, lengths, 0))
    block_rows = tokens.shape[1] // 2
    within = jnp.arange(block_rows, dtype=jnp.int32)

    def block_positions(flip_row, flip_col):
        return (2 * (row ^ flip_row) + ((col & 1) ^ flip_col)) * block_rows + within

    positions = block_positions(0, 0)
    key_pos = jnp.concatenate([positions] + [block_positions(*flips) for flips in SQUARE])
    keep = (key_pos < slot_length)[:, None].astype(jnp.int32)
    cosine, sine = rotary_tables(key_pos)

    head_width = output_width
    rest_width = expand_width + shrink_width
    rest_pad = -rest_width % LANE
    first_width = 3 * head_width + LANE
    middle_width = head_width + expand_width
    shard = jnp.concatenate(
        [
            project_weight[:, 1],
            norm_gains.T,
            jnp.zeros((shard_rows, LANE - 2), F32),
            project_weight[:, 0],
            project_weight[:, 2],
            output_weight.T,
            expand_weight.reshape(shard_rows, expand_width),
            shrink_weight.T,
            jnp.zeros((shard_rows, rest_pad), F32),
        ],
        axis=1,
    ).astype(BF16)
    block = gather_x(shard)
    first_pieces = ring_pieces(by_z_first(gather_ring(block[:, :first_width], "z")), "col")

    block, tokens, cotangent = lax.optimization_barrier((block, tokens, cotangent))
    rest_block = gather_ring(block[:, first_width:], "col")
    rest_block = rest_block.reshape(-1, rest_block.shape[-1])
    columns = tokens.shape[2]
    arrived = to_chip(jnp.concatenate([tokens[0], cotangent[0]], axis=1))
    tokens_own = jnp.concatenate([piece[:, :columns] for piece in arrived], axis=1)
    cotangent_own = jnp.concatenate([piece[:, columns:] for piece in arrived], axis=1)
    tokens_all = join_cores(
        jnp.concatenate([tokens_own] + [square_move(tokens_own, *flips) for flips in SQUARE])
    )
    cotangent_chip = join_cores(cotangent_own)
    back = jnp.where(
        (positions < slot_length)[:, None], cotangent_chip, jnp.zeros_like(cotangent_chip)
    )
    centered_all, inverse_all = norm_forward(tokens_all.astype(F32))
    inputs = tokens_all[:block_rows]
    centered_one, inverse_one = centered_all[:block_rows], inverse_all[:block_rows]

    middle_gathered = lax.all_gather(rest_block[:, :middle_width], "z")
    middle_gathered = middle_gathered.reshape(4, 8, -1, middle_width)
    shrink_all = by_z_last(gather_ring(rest_block[:, middle_width:], "z"))

    features = tokens_all.shape[1]
    keys_count = tokens_all.shape[0]
    gains_block = jnp.stack([piece[:, head_width : head_width + 2] for piece in first_pieces])
    gains_order = (col - jnp.arange(4)) & 3
    onehot = (gains_order[:, None] == jnp.arange(4)[None, :]).astype(F32)
    gains_low = jnp.sum(
        onehot[:, :, None, None] * gains_block.astype(F32)[:, None], axis=0
    ).reshape(features, 2)
    gain_one, gain_two = gains_low[:, 0][None, :], gains_low[:, 1][None, :]

    first_all, normed_all, queries, pairs, attended = kernel_call(
        forward_kernel,
        [
            ((4, features // 4, first_width), BF16),
            ((keys_count, features), BF16),
            ((block_rows, head_width), BF16),
            ((keys_count, 2 * head_width), BF16),
            ((block_rows, head_width), BF16),
        ],
        col.astype(jnp.int32).reshape(1),
        *first_pieces,
        keep,
        centered_all,
        gain_one,
        cosine,
        sine,
        scalars=1,
    )
    first_all = first_all.reshape(features, first_width)
    key_low = first_all[:, :head_width]
    query_low = first_all[:, head_width + LANE : 2 * head_width + LANE]
    value_low = first_all[:, 2 * head_width + LANE :]
    middle_all, output_part = kernel_call(
        output_kernel,
        [((features, middle_width), BF16), ((block_rows, features), F32)],
        attended,
        middle_gathered,
    )
    centered_two, inverse_two, normed_two, hidden, grad_expanded, mixed_part, normed_grad_part = (
        kernel_call(
            feed_kernel,
            [
                ((block_rows, features), F32),
                ((block_rows, 1), F32),
                ((block_rows, features), BF16),
                ((block_rows, shrink_width), BF16),
                ((block_rows, expand_width), BF16),
                ((block_rows, features), F32),
                ((block_rows, features), F32),
            ],
            inputs,
            output_part,
            swap_cores(output_part),
            gain_two,
            middle_all,
            shrink_all,
            back,
        )
    )
    normed_grad_other = swap_cores(normed_grad_part)
    (rest_grad,) = kernel_call(
        rest_grads_kernel,
        [((4, 8, features // 32, rest_width + rest_pad), BF16)],
        normed_two,
        grad_expanded,
        back,
        hidden,
    )
    rest_own = lax.psum_scatter(
        rest_grad.reshape(features, -1), "z", scatter_dimension=0, tiled=True
    )
    grad_mid, query_grad, pair_grad, first_grad = pl.pallas_call(
        backward_kernel,
        out_shape=(
            jax.ShapeDtypeStruct((block_rows, features), F32),
            jax.ShapeDtypeStruct((block_rows, head_width), BF16),
            jax.ShapeDtypeStruct((keys_count, 2 * head_width), BF16),
            jax.ShapeDtypeStruct((features, 4 * head_width), BF16),
        ),
        scratch_shapes=[
            pltpu.VMEM((block_rows, head_width), F32),
            pltpu.VMEM((keys_count, head_width), F32),
        ],
        compiler_params=pltpu.CompilerParams(vmem_limit_bytes=44 * 2**20),
    )(
        keep,
        normed_grad_part,
        normed_grad_other,
        centered_two,
        inverse_two,
        gain_two,
        back,
        middle_all,
        queries,
        pairs,
        normed_all,
        attended,
        cosine,
        sine,
    )
    parts = pair_grad.reshape(4, block_rows, 2 * head_width)
    pair_total = parts[0].astype(F32)
    for index, flips in enumerate(SQUARE):
        pair_total = pair_total + square_move(parts[index + 1], *flips).astype(F32)
    pair_total = pair_total.astype(BF16)
    mixed_home = from_chip(sum_cores(mixed_part).astype(BF16))

    first_sum = exchange_sum(first_grad.reshape(4, features // 4, -1), "col")
    first_sum = jnp.swapaxes(first_sum.reshape(2, 4, features // 32, -1), 0, 1)
    first_sum = exchange_sum(first_sum.reshape(4, features // 16, -1), "z")
    rest_sum = scatter_col(rest_own).astype(BF16)
    owned = scatter_x(jnp.concatenate([first_sum, rest_sum], axis=1))

    grad_normed_one = sum_cores(
        product_turned(query_grad, query_low)
        + product_turned(pair_total[:, :head_width], key_low)
        + product_turned(pair_total[:, head_width:], value_low)
    )
    grad_input_norm, _ = norm_backward(grad_normed_one, centered_one, inverse_one, gain_one)
    grad_input = from_chip((grad_mid + grad_input_norm).astype(BF16))

    project_grad = jnp.stack(
        [
            owned[:, head_width : 2 * head_width],
            owned[:, :head_width],
            owned[:, 2 * head_width : 3 * head_width],
        ],
        axis=1,
    )
    first_owned, rest_owned = owned[:, 3 * head_width :], owned[:, 4 * head_width :]

    def gain_part(weight, grad):
        return jnp.sum(weight.astype(BF16).astype(F32) * grad, axis=(1, 2))

    expand_grad = rest_owned[:, :expand_width].reshape(expand_weight.shape)
    gain_grad = jnp.stack(
        [gain_part(project_weight, project_grad), gain_part(expand_weight, expand_grad)]
    )
    gain_grad = gain_grad + move(gain_grad, ("row",), lambda place: (place ^ 1,))
    gain_grad = gain_grad / norm_gains.astype(BF16).astype(F32)
    output_grad = first_owned[:, :output_width].T
    shrink_grad = rest_owned[:, expand_width:rest_width].T
    return (
        (mixed_home[None], grad_input[None])
        + adam_update(norm_gains, gain_grad, norm_first, norm_second, rate_gain, 0.0)
        + adam_update(
            project_weight, project_grad, project_first, project_second, rate_matrix, decay_matrix
        )
        + adam_update(
            output_weight, output_grad, output_first, output_second, rate_matrix, decay_matrix
        )
        + adam_update(
            expand_weight, expand_grad, expand_first, expand_second, rate_matrix, decay_matrix
        )
        + adam_update(
            shrink_weight, shrink_grad, shrink_first, shrink_second, rate_matrix, decay_matrix
        )
    )


def solution(mesh):
    fine = Mesh(mesh.devices.reshape(tuple(SIZES.values())), tuple(SIZES))
    dp = ("xh", "z", "core")
    owners = ("col",) + dp
    active = P(dp, "row", "col")
    gains = P(None, owners)
    features_first = P(owners, None, "row")
    features_last = P("row", owners)
    params = (gains, features_first, features_last, features_first, features_last)
    moments = tuple(spec for spec in params for _ in range(2))
    results = tuple(spec for spec in params for _ in range(4))
    return jax.shard_map(
        on_device,
        mesh=fine,
        in_specs=(active, active, P(), P()) + params + moments,
        out_specs=(active, active) + results,
        check_vma=False,
    )
```

```python
import itertools

import jax
import jax.numpy as jnp
import numpy as np
from jax import lax
from jax.experimental import pallas as pl
from jax.experimental.pallas import tpu as pltpu
from jax.sharding import Mesh, PartitionSpec as P

HEAD = 64
STEP = 10


eps_norm = 1e-05
rope_base = 160000.0
beta_one = 0.9
beta_two = 0.999
adam_eps = 1e-08
rate_matrix = 0.05
rate_gain = 0.3
decay_matrix = 0.01
masked_score = -1e30

SIZES = {"xh": 2, "z": 4, "core": 2, "row": 2, "col": 4}
LANE = 128
GRANT = 44
BF16 = jnp.bfloat16
F32 = jnp.float32


def move(value, axes, target):
    sizes = [SIZES[axis] for axis in axes]

    def flat(place):
        return int(np.ravel_multi_index(place, sizes))

    pairs = [
        (flat(place), flat(target(*place))) for place in itertools.product(*map(range, sizes))
    ]
    return lax.ppermute(value, axes, pairs)


def swap_cores(value):
    return move(value, ("core",), lambda core: (core ^ 1,))


def sum_cores(partial_value):
    return partial_value + swap_cores(partial_value)


def ordered(flag, first, second):
    return jnp.where(flag == 0, first, second), jnp.where(flag == 0, second, first)


def owner_move(value, flip):
    return move(
        value,
        ("xh", "core", "row"),
        lambda xh, core, row: (xh ^ (flip >> 1), row, core ^ (flip & 1)),
    )


def owner_return(value, flip):
    return move(
        value,
        ("xh", "core", "row"),
        lambda xh, core, row: (xh ^ (flip >> 1), row ^ (flip & 1), core),
    )


def shift(value, axis, step):
    return move(value, (axis,), lambda place: ((place + step) % SIZES[axis],))


def gather_x(shard):
    own = [owner_move(shard, flip) for flip in range(4)]
    row, xh = lax.axis_index("row"), lax.axis_index("xh")
    near = jnp.concatenate(ordered(row, own[0], own[1]), axis=0)
    far = jnp.concatenate(ordered(row, own[2], own[3]), axis=0)
    return jnp.concatenate(ordered(xh, near, far), axis=0)


def ring_pieces(block, axis):
    return [block] + [shift(block, axis, step) for step in (1, 2, 3)]


def ring_halves(block, axis):
    half = block.shape[0] // 2
    before, after = shift(block, axis, 1), shift(block, axis, 3)
    return block, before, after, shift(before[:half], axis, 1), shift(after[half:], axis, 3)


def together(*values):
    return lax.optimization_barrier(values)


def scatter_ring(blocks, axis, dim=0):
    here = lax.axis_index(axis)

    def pick_at(index):
        return lax.dynamic_index_in_dim(blocks, index, dim, keepdims=False)

    total = pick_at(here).astype(F32)
    for step in (1, 2, 3):
        total = total + shift(pick_at((here + step) % 4), axis, step).astype(F32)
    return total


def scatter_col(grad):
    rows, width = grad.shape
    return scatter_ring(grad.reshape(4, rows // 4, width), "col")


def exchange_sum(blocks, axis):
    received = lax.all_to_all(blocks, axis, split_axis=0, concat_axis=0)
    return jnp.sum(received.astype(F32), axis=0).astype(BF16)


def scatter_x(block):
    rows = block.shape[0] // 4
    row, xh = lax.axis_index("row"), lax.axis_index("xh")
    near, far = ordered(xh, block[: 2 * rows], block[2 * rows :])
    pieces = ordered(row, near[:rows], near[rows:]) + ordered(row, far[:rows], far[rows:])
    return sum(owner_return(piece, flip).astype(F32) for flip, piece in enumerate(pieces))


def chip_move(value, flip):
    return move(
        value, ("core", "col"), lambda core, col: (col >> 1, 2 * core + ((col & 1) ^ flip))
    )


def to_chip(value):
    odd = lax.axis_index("col") & 1
    rows = value.shape[0] // 2
    halves = ordered(odd, value[:rows], value[rows:])
    return ordered(odd, *[chip_move(half, flip) for flip, half in enumerate(halves)])


def join_cores(value):
    return jnp.concatenate(ordered(lax.axis_index("core"), value, swap_cores(value)), axis=1)


def from_chip(*values):
    core, odd = lax.axis_index("core"), lax.axis_index("col") & 1
    half = values[0].shape[1] // 2
    mine = [jnp.where(core == 0, value[:, :half], value[:, half:]) for value in values]
    pieces = ordered(
        odd,
        jnp.concatenate([value[:, : half // 2] for value in mine], axis=1),
        jnp.concatenate([value[:, half // 2 :] for value in mine], axis=1),
    )
    received = [chip_move(piece, flip) for flip, piece in enumerate(pieces)]
    home = jnp.concatenate(ordered(odd, *received), axis=0)
    return tuple(jnp.split(home, len(values), axis=1))


SQUARE = ((1, 0), (0, 1), (1, 1))


def square_move(value, flip_row, flip_col):
    return move(value, ("row", "col"), lambda row, col: (row ^ flip_row, col ^ flip_col))


def rotary_tables(positions):
    half = HEAD // 2
    freqs = rope_base ** (-(2.0 * jnp.arange(half, dtype=F32)) / HEAD)
    angles = positions.astype(F32)[:, None] * freqs[None, :]
    cosine, sine = jnp.cos(angles), jnp.sin(angles)
    return (
        jnp.concatenate([cosine] * 4, axis=-1),
        jnp.concatenate([-sine, sine, -sine, sine], axis=-1),
    )


def turned(values):
    lane = lax.broadcasted_iota(jnp.int32, values.shape, 1)
    first = lane % HEAD < HEAD // 2
    back, ahead = pltpu.roll(values, LANE - HEAD // 2, 1), pltpu.roll(values, HEAD // 2, 1)
    return jnp.where(first, back, ahead)


def product(left, right):
    return lax.dot_general(left, right, (((1,), (0,)), ((), ())), preferred_element_type=F32)


def product_turned(left, right):
    return lax.dot_general(left, right, (((1,), (1,)), ((), ())), preferred_element_type=F32)


def token_product(left, right):
    return lax.dot_general(left, right, (((0,), (0,)), ((), ())), preferred_element_type=F32)


def norm_forward(value):
    count = value.shape[-1]
    average = jnp.sum(value, axis=-1, keepdims=True) / count
    spread = jnp.sum(value * value, axis=-1, keepdims=True) / count - average * average
    inverse = lax.rsqrt(spread + eps_norm)
    return ((value - average) * inverse, inverse)


def norm_backward(grad_out, centered, inverse, gain):
    count = grad_out.shape[-1]
    scaled = grad_out * gain
    total = jnp.sum(scaled, axis=-1, keepdims=True)
    along = jnp.sum(scaled * centered, axis=-1, keepdims=True)
    grad_value = inverse * (scaled - total / count - centered * (along / count))
    grad_gain = jnp.sum(grad_out * centered, axis=0)
    return (grad_value, grad_gain)


def adam_update(param, grad, first, second, rate, decay):
    first_new = beta_one * first + (1.0 - beta_one) * grad
    second_new = beta_two * second + (1.0 - beta_two) * grad * grad
    mean_hat = first_new / (1.0 - beta_one**STEP)
    square_hat = second_new / (1.0 - beta_two**STEP)
    fresh = param - rate * (mean_hat / (jnp.sqrt(square_hat) + adam_eps) + decay * param)
    return (grad, first_new, second_new, fresh)


def kernel_dot(left, right, left_dim, right_dim):
    return lax.dot_general(
        left, right, (((left_dim,), (right_dim,)), ((), ())), preferred_element_type=F32
    )


def kernel_call(body, shapes, *operands, scratch=(), grant=GRANT, scalars=0):
    return pl.pallas_call(
        body,
        out_shape=tuple(jax.ShapeDtypeStruct(*shape) for shape in shapes),
        in_specs=[pl.BlockSpec(memory_space=pltpu.SMEM)] * scalars
        + [pl.BlockSpec(memory_space=pltpu.VMEM)] * (len(operands) - scalars),
        scratch_shapes=[pltpu.VMEM(*shape) for shape in scratch],
        compiler_params=pltpu.CompilerParams(vmem_limit_bytes=grant * 2**20),
    )(*operands)


def softmax_turned(keep, key, query):
    scores = jnp.where(keep, kernel_dot(key, query, 1, 1) * HEAD ** (-0.5), masked_score)
    exps = jnp.exp(scores - jnp.max(scores, axis=0, keepdims=True))
    return exps * (1.0 / jnp.sum(exps, axis=0, keepdims=True))


def forward_kernel(
    place_ref,
    piece_own,
    piece_before,
    piece_after,
    far_first,
    far_last,
    keep_ref,
    centered_ref,
    cosine_ref,
    sine_ref,
    weight_out,
    gains_out,
    normed_out,
    query_out,
    pair_out,
    attended_out,
):
    width = query_out.shape[1]
    rows = query_out.shape[0]
    for hop in range(4):
        half = far_first.shape[0]
        far = (far_first, hop) if hop < half else (far_last, hop - half)
        pieces = ((piece_own, hop), (piece_before, hop), far, (piece_after, hop))
        for step, (piece, index) in enumerate(pieces):
            at = (place_ref[0] - step) & 3, (place_ref[1] - hop) & 3
            put_rows(weight_out, *at, piece, index)
    weight = as_rows(weight_out)
    gains = weight[:, width : width + LANE].astype(F32).T
    gains_out[...] = gains[: gains_out.shape[0]]
    gain = gains[:1]
    normed_out[...] = (centered_ref[...] * gain).astype(BF16)
    normed = normed_out[...]
    query_at, value_at = width + LANE, 2 * width + LANE

    def rotated(values, count):
        return (values * cosine_ref[:count] + turned(values) * sine_ref[:count]).astype(BF16)

    for start in range(0, width, LANE):
        at = slice(start, start + LANE)
        pair_out[:, at] = rotated(kernel_dot(normed, weight[:, at], 1, 0), normed.shape[0])
        query_weight = weight[:, query_at + start : query_at + start + LANE]
        query_out[:, at] = rotated(kernel_dot(normed[:rows], query_weight, 1, 0), rows)
    value_weight = weight[:, value_at : value_at + width]
    pair_out[:, width:] = kernel_dot(normed, value_weight, 1, 0).astype(BF16)
    keep = keep_ref[...] > 0
    for head in range(width // HEAD):
        at = slice(HEAD * head, HEAD * (head + 1))
        values = pair_out[:, width + HEAD * head : width + HEAD * (head + 1)]
        probs_low = softmax_turned(keep, pair_out[:, at], query_out[:, at]).astype(BF16)
        attended_out[:, at] = kernel_dot(probs_low, values, 0, 0).astype(BF16)


def put_rows(ordered_ref, col, z, source, *at):
    part = ordered_ref.shape[3]
    lead, columns = at[:-1], at[-1]
    if not isinstance(columns, slice):
        lead, columns = at, slice(None)
    for xh in range(2):
        ordered_ref[col, xh, z] = source[(*lead, slice(xh * part, (xh + 1) * part), columns)]


def as_rows(ordered_ref):
    return ordered_ref[...].reshape(-1, ordered_ref.shape[-1])


def put_by_z(result, out_ref, start):
    part = out_ref.shape[2]
    for group in range(4 * out_ref.shape[1]):
        out_ref[group % 4, group // 4, :, start : start + result.shape[1]] = result[
            group * part : (group + 1) * part
        ]


def output_kernel(
    place_ref,
    attended_ref,
    gathered_ref,
    weight_out,
    shrink_out,
    part_out,
):
    split = weight_out.shape[4]
    for step in range(4):
        for z in range(4):
            at = (place_ref[0] - step) & 3, z
            put_rows(weight_out, *at, gathered_ref, z, step, slice(0, split))
            put_rows(
                shrink_out, *at, gathered_ref, z, step, slice(split, gathered_ref.shape[3])
            )
    width = attended_ref.shape[1]
    part_out[...] = kernel_dot(attended_ref[...], as_rows(weight_out)[:, :width], 1, 1)


def feed_kernel(
    input_ref,
    part_ref,
    other_ref,
    gain_ref,
    weight_ref,
    shrink_ref,
    back_ref,
    centered_out,
    inverse_out,
    normed_out,
    hidden_out,
    grad_out,
    mixed_out,
    normed_grad_out,
):
    units = hidden_out.shape[1]
    middle = input_ref[...].astype(F32) + (part_ref[...] + other_ref[...])
    centered, inverse = norm_forward(middle)
    centered_out[...] = centered
    inverse_out[...] = inverse
    normed = (centered * gain_ref[...]).astype(BF16)
    normed_out[...] = normed
    expand = weight_ref[:, weight_ref.shape[1] - 2 * units :]
    shrink = shrink_ref[:, :units]
    expanded = kernel_dot(normed, expand, 1, 0)
    active, gate = expanded[:, :units], expanded[:, units:]
    phi = 0.5 * (1.0 + lax.erf(active * 0.5**0.5))
    density = jnp.exp(-0.5 * active * active) * (2.0 * np.pi) ** (-0.5)
    gelu = active * phi
    hidden = (gelu * gate).astype(BF16)
    hidden_out[...] = hidden
    mixed_out[...] = 0.5 * middle + kernel_dot(hidden, shrink, 1, 1)
    grad_hidden = kernel_dot(back_ref[...], shrink, 1, 0)
    grad_out[:, :units] = (grad_hidden * gate * (phi + active * density)).astype(BF16)
    grad_out[:, units:] = (grad_hidden * gelu).astype(BF16)
    normed_grad_out[...] = kernel_dot(grad_out[...], expand, 1, 1)


def rest_grads_kernel(normed_ref, grad_ref, back_ref, hidden_ref, out_ref):
    expand_width, units = grad_ref.shape[1], hidden_ref.shape[1]
    put_by_z(kernel_dot(normed_ref[...], grad_ref[...], 0, 0).astype(BF16), out_ref, 0)
    put_by_z(
        kernel_dot(back_ref[...], hidden_ref[...], 0, 0).astype(BF16), out_ref, expand_width
    )
    pad = out_ref.shape[3] - expand_width - units
    put_by_z(jnp.zeros((normed_ref.shape[1], pad), BF16), out_ref, expand_width + units)


def backward_kernel(
    keep_ref,
    part_ref,
    other_ref,
    centered_ref,
    inverse_ref,
    gain_ref,
    back_ref,
    weight_ref,
    query_ref,
    pair_ref,
    normed_ref,
    attended_ref,
    cosine_ref,
    sine_ref,
    middle_out,
    query_out,
    pair_out,
    grads_out,
    query_grad,
    key_grad,
):
    width = query_ref.shape[1]
    rows = query_ref.shape[0]
    grad_norm, _ = norm_backward(
        part_ref[...] + other_ref[...], centered_ref[...], inverse_ref[...], gain_ref[...]
    )
    grad_middle = back_ref[...].astype(F32) + grad_norm
    middle_out[...] = grad_middle
    middle_low = grad_middle.astype(BF16)
    grad_attended = kernel_dot(middle_low, weight_ref[:, :width], 1, 0).astype(BF16)
    keep = keep_ref[...] > 0
    for head in range(width // HEAD):
        at = slice(HEAD * head, HEAD * (head + 1))
        value_at = slice(width + HEAD * head, width + HEAD * (head + 1))
        query, grad = query_ref[:, at], grad_attended[:, at]
        key, value = pair_ref[:, at], pair_ref[:, value_at]
        probs = softmax_turned(keep, key, query)
        grad_probs = kernel_dot(value, grad, 1, 1)
        centre = jnp.sum(probs * grad_probs, axis=0, keepdims=True)
        grad_raw = (probs * (grad_probs - centre) * HEAD ** (-0.5)).astype(BF16)
        query_grad[:, at] = kernel_dot(grad_raw, key, 0, 0)
        key_grad[:, at] = kernel_dot(grad_raw, query, 1, 0)
        pair_out[:, value_at] = kernel_dot(probs.astype(BF16), grad, 1, 0).astype(BF16)

    def unrotated(values, count):
        return (values * cosine_ref[:count] - turned(values) * sine_ref[:count]).astype(BF16)

    for start in range(0, width, LANE):
        at = slice(start, start + LANE)
        query_out[:, at] = unrotated(query_grad[:, at], rows)
        pair_out[:, at] = unrotated(key_grad[:, at], key_grad.shape[0])
    normed = normed_ref[...]
    put_by_z(kernel_dot(normed, pair_out[...], 0, 0).astype(BF16), grads_out, 0)
    put_by_z(
        kernel_dot(normed[:rows], query_out[...], 0, 0).astype(BF16), grads_out, 2 * width
    )
    put_by_z(kernel_dot(middle_low, attended_ref[...], 0, 0).astype(BF16), grads_out, 3 * width)


def on_device(
    tokens,
    cotangent,
    lengths,
    assign,
    norm_gains,
    project_weight,
    output_weight,
    expand_weight,
    shrink_weight,
    norm_first,
    norm_second,
    project_first,
    project_second,
    output_first,
    output_second,
    expand_first,
    expand_second,
    shrink_first,
    shrink_second,
):
    row, col = lax.axis_index("row"), lax.axis_index("col")
    shard_rows = project_weight.shape[0]
    output_width = output_weight.shape[0]
    expand_width = 2 * expand_weight.shape[2]
    shrink_width = shrink_weight.shape[0]
    heads_here = output_width // HEAD

    slot = (lax.axis_index("xh") * 4 + lax.axis_index("z")) * 2 + (col >> 1)
    catalog = jnp.arange(lengths.shape[0], dtype=jnp.int32)
    seq_id = jnp.sum(jnp.where(catalog == slot, assign, 0))
    slot_length = jnp.sum(jnp.where(catalog == seq_id, lengths, 0))
    block_rows = tokens.shape[1] // 2
    within = jnp.arange(block_rows, dtype=jnp.int32)

    def block_positions(flip_row, flip_col):
        return (2 * (row ^ flip_row) + ((col & 1) ^ flip_col)) * block_rows + within

    positions = block_positions(0, 0)
    key_pos = jnp.concatenate([positions] + [block_positions(*flips) for flips in SQUARE])
    keep = (key_pos < slot_length)[:, None].astype(jnp.int32)
    cosine, sine = rotary_tables(key_pos)

    head_width = output_width
    rest_width = expand_width + shrink_width
    rest_pad = -rest_width % LANE
    first_width = 3 * head_width + LANE
    middle_width = head_width + expand_width
    shard = jnp.concatenate(
        [
            project_weight[:, 1],
            norm_gains.T,
            jnp.zeros((shard_rows, LANE - 2), F32),
            project_weight[:, 0],
            project_weight[:, 2],
            output_weight.T,
            expand_weight.reshape(shard_rows, expand_width),
            shrink_weight.T,
            jnp.zeros((shard_rows, rest_pad), F32),
        ],
        axis=1,
    ).astype(BF16)
    columns = tokens.shape[2]
    arrived = to_chip(jnp.concatenate([tokens[0], cotangent[0]], axis=1))
    block = gather_x(shard)
    first_pieces = ring_pieces(block[:, :first_width], "z")
    rest_pieces = ring_pieces(block[:, first_width:], "col")
    stages = together(*first_pieces, *rest_pieces)
    first_pieces = ring_halves(jnp.stack(stages[:4]), "col")
    rest_gathered = lax.all_gather(jnp.stack(stages[4:]), "z")
    tokens_own = jnp.concatenate([piece[:, :columns] for piece in arrived], axis=1)
    tokens_half = [tokens_own] + [square_move(tokens_own, *flips) for flips in SQUARE]
    cotangent_own = jnp.concatenate([piece[:, columns:] for piece in arrived], axis=1)
    tokens_all = join_cores(jnp.concatenate(tokens_half))
    cotangent_chip = join_cores(cotangent_own)
    back = jnp.where(
        (positions < slot_length)[:, None], cotangent_chip, jnp.zeros_like(cotangent_chip)
    )
    centered_all, inverse_all = norm_forward(tokens_all.astype(F32))
    inputs = tokens_all[:block_rows]
    centered_one, inverse_one = centered_all[:block_rows], inverse_all[:block_rows]

    features = tokens_all.shape[1]
    keys_count = tokens_all.shape[0]
    place = jnp.stack([col, lax.axis_index("z")]).astype(jnp.int32)
    first_all, gains_low, normed_all, queries, pairs, attended = kernel_call(
        forward_kernel,
        [
            ((4, 2, 4, features // 32, first_width), BF16),
            ((8, features), F32),
            ((keys_count, features), BF16),
            ((block_rows, head_width), BF16),
            ((keys_count, 2 * head_width), BF16),
            ((block_rows, head_width), BF16),
        ],
        place,
        *first_pieces,
        keep,
        centered_all,
        cosine,
        sine,
        scalars=1,
    )
    first_all = first_all.reshape(features, first_width)
    gain_one, gain_two = gains_low[:1], gains_low[1:2]
    key_low = first_all[:, :head_width]
    query_low = first_all[:, head_width + LANE : 2 * head_width + LANE]
    value_low = first_all[:, 2 * head_width + LANE :]
    middle_all, shrink_all, output_part = kernel_call(
        output_kernel,
        [
            ((4, 2, 4, features // 32, middle_width), BF16),
            ((4, 2, 4, features // 32, shrink_width + rest_pad), BF16),
            ((block_rows, features), F32),
        ],
        place,
        attended,
        rest_gathered,
        scalars=1,
    )
    middle_all = middle_all.reshape(features, -1)
    shrink_all = shrink_all.reshape(features, -1)
    centered_two, inverse_two, normed_two, hidden, grad_expanded, mixed_part, normed_grad_part = (
        kernel_call(
            feed_kernel,
            [
                ((block_rows, features), F32),
                ((block_rows, 1), F32),
                ((block_rows, features), BF16),
                ((block_rows, shrink_width), BF16),
                ((block_rows, expand_width), BF16),
                ((block_rows, features), F32),
                ((block_rows, features), F32),
            ],
            inputs,
            output_part,
            swap_cores(output_part),
            gain_two,
            middle_all,
            shrink_all,
            back,
        )
    )
    normed_grad_other = swap_cores(normed_grad_part)
    (rest_grad,) = kernel_call(
        rest_grads_kernel,
        [((4, 8, features // 32, rest_width + rest_pad), BF16)],
        normed_two,
        grad_expanded,
        back,
        hidden,
    )
    rest_own = lax.psum_scatter(
        rest_grad.reshape(features, -1), "z", scatter_dimension=0, tiled=True
    )
    normed_grad_other, rest_grad = together(normed_grad_other, rest_grad)
    grad_mid, query_grad, pair_grad, first_grad = kernel_call(
        backward_kernel,
        [
            ((block_rows, features), F32),
            ((block_rows, head_width), BF16),
            ((keys_count, 2 * head_width), BF16),
            ((4, 8, features // 32, 4 * head_width), BF16),
        ],
        keep,
        normed_grad_part,
        normed_grad_other,
        centered_two,
        inverse_two,
        gain_two,
        back,
        middle_all,
        queries,
        pairs,
        normed_all,
        attended,
        cosine,
        sine,
        scratch=[((block_rows, head_width), F32), ((keys_count, head_width), F32)],
    )
    first_sum = exchange_sum(first_grad.reshape(4, features // 4, -1), "z")
    rest_sum = scatter_col(rest_own).astype(BF16)
    pair_grad, rest_sum = together(pair_grad, rest_sum)
    parts = pair_grad.reshape(4, block_rows, 2 * head_width)
    received = [square_move(parts[index + 1], *flips) for index, flips in enumerate(SQUARE)]
    first_sum, rest_sum, mixed_part = together(first_sum, rest_sum, mixed_part)
    received = together(first_sum, *received)[1:]
    first_sum = exchange_sum(first_sum.reshape(4, features // 16, -1), "col")
    owned_part = jnp.concatenate([first_sum, rest_sum], axis=1)
    pair_total = sum((piece.astype(F32) for piece in received), parts[0].astype(F32))
    pair_total = pair_total.astype(BF16)

    grad_normed_one = sum_cores(
        product_turned(query_grad, query_low)
        + product_turned(pair_total[:, :head_width], key_low)
        + product_turned(pair_total[:, head_width:], value_low)
    )
    grad_input_norm, _ = norm_backward(grad_normed_one, centered_one, inverse_one, gain_one)
    grad_input_chip = (grad_mid + grad_input_norm).astype(BF16)
    mixed_chip = sum_cores(mixed_part).astype(BF16)
    owned_part, grad_input_chip, mixed_chip = together(owned_part, grad_input_chip, mixed_chip)
    owned = scatter_x(owned_part)
    mixed_home, grad_input = from_chip(mixed_chip, grad_input_chip)

    project_grad = jnp.stack(
        [
            owned[:, 2 * head_width : 3 * head_width],
            owned[:, :head_width],
            owned[:, head_width : 2 * head_width],
        ],
        axis=1,
    )
    first_owned, rest_owned = owned[:, 3 * head_width :], owned[:, 4 * head_width :]

    def gain_part(weight, grad):
        return jnp.sum(weight.astype(BF16).astype(F32) * grad, axis=(1, 2))

    expand_grad = rest_owned[:, :expand_width].reshape(expand_weight.shape)
    gain_grad = jnp.stack(
        [gain_part(project_weight, project_grad), gain_part(expand_weight, expand_grad)]
    )
    gain_grad = gain_grad + move(gain_grad, ("row",), lambda place: (place ^ 1,))
    gain_grad = gain_grad / norm_gains.astype(BF16).astype(F32)
    output_grad = first_owned[:, :output_width].T
    shrink_grad = rest_owned[:, expand_width:rest_width].T
    return (
        (mixed_home[None], grad_input[None])
        + adam_update(norm_gains, gain_grad, norm_first, norm_second, rate_gain, 0.0)
        + adam_update(
            project_weight, project_grad, project_first, project_second, rate_matrix, decay_matrix
        )
        + adam_update(
            output_weight, output_grad, output_first, output_second, rate_matrix, decay_matrix
        )
        + adam_update(
            expand_weight, expand_grad, expand_first, expand_second, rate_matrix, decay_matrix
        )
        + adam_update(
            shrink_weight, shrink_grad, shrink_first, shrink_second, rate_matrix, decay_matrix
        )
    )


def solution(mesh):
    fine = Mesh(mesh.devices.reshape(tuple(SIZES.values())), tuple(SIZES))
    dp = ("xh", "z", "core")
    owners = ("col",) + dp
    active = P(dp, "row", "col")
    gains = P(None, owners)
    features_first = P(owners, None, "row")
    features_last = P("row", owners)
    params = (gains, features_first, features_last, features_first, features_last)
    moments = tuple(spec for spec in params for _ in range(2))
    results = tuple(spec for spec in params for _ in range(4))
    return jax.shard_map(
        on_device,
        mesh=fine,
        in_specs=(active, active, P(), P()) + params + moments,
        out_specs=(active, active) + results,
        check_vma=False,
    )
```

```python
import itertools

import jax
import jax.numpy as jnp
import numpy as np
from jax import lax
from jax.experimental import pallas as pl
from jax.experimental.pallas import tpu as pltpu
from jax.sharding import Mesh, PartitionSpec as P

HEAD = 64
STEP = 10


eps_norm = 1e-05
rope_base = 160000.0
beta_one = 0.9
beta_two = 0.999
adam_eps = 1e-08
rate_matrix = 0.05
rate_gain = 0.3
decay_matrix = 0.01
masked_score = -1e30

SIZES = {"xh": 2, "z": 4, "core": 2, "row": 2, "col": 4}
LANE = 128
GRANT = 44
WIDE_GRANT = 58
BF16 = jnp.bfloat16
F32 = jnp.float32


def move(value, axes, target):
    sizes = [SIZES[axis] for axis in axes]

    def flat(place):
        return int(np.ravel_multi_index(place, sizes))

    pairs = [
        (flat(place), flat(target(*place))) for place in itertools.product(*map(range, sizes))
    ]
    return lax.ppermute(value, axes, pairs)


def swap_cores(value):
    return move(value, ("core",), lambda core: (core ^ 1,))


def sum_cores(partial_value):
    return partial_value + swap_cores(partial_value)


def ordered(flag, first, second):
    return jnp.where(flag == 0, first, second), jnp.where(flag == 0, second, first)


def owner_move(value, flip):
    return move(
        value,
        ("xh", "core", "row"),
        lambda xh, core, row: (xh ^ (flip >> 1), row, core ^ (flip & 1)),
    )


def owner_return(value, flip):
    return move(
        value,
        ("xh", "core", "row"),
        lambda xh, core, row: (xh ^ (flip >> 1), row ^ (flip & 1), core),
    )


def shift(value, axis, step):
    return move(value, (axis,), lambda place: ((place + step) % SIZES[axis],))


def gather_x(shard):
    own = [owner_move(shard, flip) for flip in range(4)]
    row, xh = lax.axis_index("row"), lax.axis_index("xh")
    near = jnp.concatenate(ordered(row, own[0], own[1]), axis=0)
    far = jnp.concatenate(ordered(row, own[2], own[3]), axis=0)
    return jnp.concatenate(ordered(xh, near, far), axis=0)


def ring_pieces(block, axis):
    return [block] + [shift(block, axis, step) for step in (1, 2, 3)]


def ring_halves(block, axis):
    half = block.shape[0] // 2
    before, after = shift(block, axis, 1), shift(block, axis, 3)
    return block, before, after, shift(before[:half], axis, 1), shift(after[half:], axis, 3)


def together(*values):
    return lax.optimization_barrier(values)


def scatter_ring(blocks, axis, dim=0):
    here = lax.axis_index(axis)

    def pick_at(index):
        return lax.dynamic_index_in_dim(blocks, index, dim, keepdims=False)

    total = pick_at(here).astype(F32)
    for step in (1, 2, 3):
        total = total + shift(pick_at((here + step) % 4), axis, step).astype(F32)
    return total


def scatter_col(grad):
    rows, width = grad.shape
    return scatter_ring(grad.reshape(4, rows // 4, width), "col")


def exchange_sum(blocks, axis):
    received = lax.all_to_all(blocks, axis, split_axis=0, concat_axis=0)
    return jnp.sum(received.astype(F32), axis=0).astype(BF16)


def scatter_x(block):
    rows = block.shape[0] // 4
    row, xh = lax.axis_index("row"), lax.axis_index("xh")
    near, far = ordered(xh, block[: 2 * rows], block[2 * rows :])
    pieces = ordered(row, near[:rows], near[rows:]) + ordered(row, far[:rows], far[rows:])
    return sum(owner_return(piece, flip).astype(F32) for flip, piece in enumerate(pieces))


def chip_move(value, flip):
    return move(
        value, ("core", "col"), lambda core, col: (col >> 1, 2 * core + ((col & 1) ^ flip))
    )


def to_chip(value):
    odd = lax.axis_index("col") & 1
    rows = value.shape[0] // 2
    halves = ordered(odd, value[:rows], value[rows:])
    return ordered(odd, *[chip_move(half, flip) for flip, half in enumerate(halves)])


def join_cores(value):
    return jnp.concatenate(ordered(lax.axis_index("core"), value, swap_cores(value)), axis=1)


def from_chip(*values):
    core, odd = lax.axis_index("core"), lax.axis_index("col") & 1
    half = values[0].shape[1] // 2
    mine = [jnp.where(core == 0, value[:, :half], value[:, half:]) for value in values]
    pieces = ordered(
        odd,
        jnp.concatenate([value[:, : half // 2] for value in mine], axis=1),
        jnp.concatenate([value[:, half // 2 :] for value in mine], axis=1),
    )
    received = [chip_move(piece, flip) for flip, piece in enumerate(pieces)]
    home = jnp.concatenate(ordered(odd, *received), axis=0)
    return tuple(jnp.split(home, len(values), axis=1))


SQUARE = ((1, 0), (0, 1), (1, 1))


def square_move(value, flip_row, flip_col):
    return move(value, ("row", "col"), lambda row, col: (row ^ flip_row, col ^ flip_col))


def rotary_tables(positions):
    half = HEAD // 2
    freqs = rope_base ** (-(2.0 * jnp.arange(half, dtype=F32)) / HEAD)
    angles = positions.astype(F32)[:, None] * freqs[None, :]
    cosine, sine = jnp.cos(angles), jnp.sin(angles)
    return (
        jnp.concatenate([cosine] * 4, axis=-1),
        jnp.concatenate([-sine, sine, -sine, sine], axis=-1),
    )


def turned(values):
    lane = lax.broadcasted_iota(jnp.int32, values.shape, 1)
    first = lane % HEAD < HEAD // 2
    back, ahead = pltpu.roll(values, LANE - HEAD // 2, 1), pltpu.roll(values, HEAD // 2, 1)
    return jnp.where(first, back, ahead)


def product(left, right):
    return lax.dot_general(left, right, (((1,), (0,)), ((), ())), preferred_element_type=F32)


def product_turned(left, right):
    return lax.dot_general(left, right, (((1,), (1,)), ((), ())), preferred_element_type=F32)


def token_product(left, right):
    return lax.dot_general(left, right, (((0,), (0,)), ((), ())), preferred_element_type=F32)


def norm_forward(value):
    count = value.shape[-1]
    average = jnp.sum(value, axis=-1, keepdims=True) / count
    spread = jnp.sum(value * value, axis=-1, keepdims=True) / count - average * average
    inverse = lax.rsqrt(spread + eps_norm)
    return ((value - average) * inverse, inverse)


def norm_backward(grad_out, centered, inverse, gain):
    count = grad_out.shape[-1]
    scaled = grad_out * gain
    total = jnp.sum(scaled, axis=-1, keepdims=True)
    along = jnp.sum(scaled * centered, axis=-1, keepdims=True)
    grad_value = inverse * (scaled - total / count - centered * (along / count))
    grad_gain = jnp.sum(grad_out * centered, axis=0)
    return (grad_value, grad_gain)


def adam_update(param, grad, first, second, rate, decay):
    first_new = beta_one * first + (1.0 - beta_one) * grad
    second_new = beta_two * second + (1.0 - beta_two) * grad * grad
    mean_hat = first_new / (1.0 - beta_one**STEP)
    square_hat = second_new / (1.0 - beta_two**STEP)
    fresh = param - rate * (mean_hat / (jnp.sqrt(square_hat) + adam_eps) + decay * param)
    return (grad, first_new, second_new, fresh)


def kernel_dot(left, right, left_dim, right_dim):
    return lax.dot_general(
        left, right, (((left_dim,), (right_dim,)), ((), ())), preferred_element_type=F32
    )


def kernel_call(body, shapes, *operands, scratch=(), grant=GRANT, scalars=0):
    return pl.pallas_call(
        body,
        out_shape=tuple(jax.ShapeDtypeStruct(*shape) for shape in shapes),
        in_specs=[pl.BlockSpec(memory_space=pltpu.SMEM)] * scalars
        + [pl.BlockSpec(memory_space=pltpu.VMEM)] * (len(operands) - scalars),
        scratch_shapes=[pltpu.VMEM(*shape) for shape in scratch],
        compiler_params=pltpu.CompilerParams(vmem_limit_bytes=grant * 2**20),
    )(*operands)


def softmax_turned(keep, key, query):
    scores = jnp.where(keep, kernel_dot(key, query, 1, 1), masked_score)
    exps = jnp.exp(scores - jnp.max(scores, axis=0, keepdims=True))
    return exps * (1.0 / jnp.sum(exps, axis=0, keepdims=True))


def forward_kernel(
    place_ref,
    piece_own,
    piece_before,
    piece_after,
    far_first,
    far_last,
    keep_ref,
    centered_ref,
    cosine_ref,
    sine_ref,
    weight_out,
    gains_out,
    normed_out,
    query_out,
    pair_out,
    attended_out,
):
    width = query_out.shape[1]
    rows = query_out.shape[0]
    for hop in range(4):
        half = far_first.shape[0]
        far = (far_first, hop) if hop < half else (far_last, hop - half)
        pieces = ((piece_own, hop), (piece_before, hop), far, (piece_after, hop))
        for step, (piece, index) in enumerate(pieces):
            at = (place_ref[0] - step) & 3, (place_ref[1] - hop) & 3
            put_rows(weight_out, *at, piece, index)
    weight = as_rows(weight_out)
    gains = weight[:, width : width + LANE].astype(F32).T
    gains_out[...] = gains[: gains_out.shape[0]]
    gain = gains[:1]
    normed_out[...] = (centered_ref[...] * gain).astype(BF16)
    normed = normed_out[...]
    query_at, value_at = width + LANE, 2 * width + LANE

    def rotated(values, count):
        return (values * cosine_ref[:count] + turned(values) * sine_ref[:count]).astype(BF16)

    for start in range(0, width, LANE):
        at = slice(start, start + LANE)
        pair_out[:, at] = rotated(kernel_dot(normed, weight[:, at], 1, 0), normed.shape[0])
        query_weight = weight[:, query_at + start : query_at + start + LANE]
        query_out[:, at] = rotated(kernel_dot(normed[:rows], query_weight, 1, 0), rows)
    value_weight = weight[:, value_at : value_at + width]
    pair_out[:, width:] = kernel_dot(normed, value_weight, 1, 0).astype(BF16)
    keep = keep_ref[...] > 0
    for head in range(width // HEAD):
        at = slice(HEAD * head, HEAD * (head + 1))
        values = pair_out[:, width + HEAD * head : width + HEAD * (head + 1)]
        query = query_out[:, at] * HEAD ** (-0.5)
        probs_low = softmax_turned(keep, pair_out[:, at], query).astype(BF16)
        attended_out[:, at] = kernel_dot(probs_low, values, 0, 0).astype(BF16)


def put_rows(ordered_ref, col, z, source, *at):
    part = ordered_ref.shape[3]
    lead, columns = at[:-1], at[-1]
    if not isinstance(columns, slice):
        lead, columns = at, slice(None)
    for xh in range(2):
        ordered_ref[col, xh, z] = source[(*lead, slice(xh * part, (xh + 1) * part), columns)]


def as_rows(ordered_ref):
    return ordered_ref[...].reshape(-1, ordered_ref.shape[-1])


def put_by_z(result, out_ref, start):
    part = out_ref.shape[2]
    for group in range(4 * out_ref.shape[1]):
        out_ref[group % 4, group // 4, :, start : start + result.shape[1]] = result[
            group * part : (group + 1) * part
        ]


def output_kernel(
    place_ref,
    attended_ref,
    gathered_ref,
    weight_out,
    shrink_out,
    part_out,
):
    split = weight_out.shape[4]
    for step in range(4):
        for z in range(4):
            at = (place_ref[0] - step) & 3, z
            put_rows(weight_out, *at, gathered_ref, z, step, slice(0, split))
            put_rows(
                shrink_out, *at, gathered_ref, z, step, slice(split, gathered_ref.shape[3])
            )
    width = attended_ref.shape[1]
    part_out[...] = kernel_dot(attended_ref[...], as_rows(weight_out)[:, :width], 1, 1)


def feed_kernel(
    input_ref,
    part_ref,
    other_ref,
    gain_ref,
    weight_ref,
    shrink_ref,
    back_ref,
    centered_out,
    inverse_out,
    normed_out,
    hidden_out,
    grad_out,
    mixed_out,
    normed_grad_out,
):
    units = hidden_out.shape[1]
    middle = input_ref[...].astype(F32) + (part_ref[...] + other_ref[...])
    centered, inverse = norm_forward(middle)
    centered_out[...] = centered
    inverse_out[...] = inverse
    normed = (centered * gain_ref[...]).astype(BF16)
    normed_out[...] = normed
    expand = weight_ref[:, weight_ref.shape[1] - 2 * units :]
    shrink = shrink_ref[:, :units]
    expanded = kernel_dot(normed, expand, 1, 0)
    active, gate = expanded[:, :units], expanded[:, units:]
    phi = 0.5 * (1.0 + lax.erf(active * 0.5**0.5))
    density = jnp.exp(-0.5 * active * active) * (2.0 * np.pi) ** (-0.5)
    gelu = active * phi
    hidden = (gelu * gate).astype(BF16)
    hidden_out[...] = hidden
    mixed_out[...] = 0.5 * middle + kernel_dot(hidden, shrink, 1, 1)
    grad_hidden = kernel_dot(back_ref[...], shrink, 1, 0)
    grad_out[:, :units] = (grad_hidden * gate * (phi + active * density)).astype(BF16)
    grad_out[:, units:] = (grad_hidden * gelu).astype(BF16)
    normed_grad_out[...] = kernel_dot(grad_out[...], expand, 1, 1)


def rest_grads_kernel(normed_ref, grad_ref, back_ref, hidden_ref, out_ref):
    expand_width, units = grad_ref.shape[1], hidden_ref.shape[1]
    put_by_z(kernel_dot(normed_ref[...], grad_ref[...], 0, 0).astype(BF16), out_ref, 0)
    put_by_z(
        kernel_dot(back_ref[...], hidden_ref[...], 0, 0).astype(BF16), out_ref, expand_width
    )
    pad = out_ref.shape[3] - expand_width - units
    put_by_z(jnp.zeros((normed_ref.shape[1], pad), BF16), out_ref, expand_width + units)


def backward_kernel(
    keep_ref,
    part_ref,
    other_ref,
    centered_ref,
    inverse_ref,
    gain_ref,
    back_ref,
    weight_ref,
    query_ref,
    pair_ref,
    normed_ref,
    attended_ref,
    cosine_ref,
    sine_ref,
    middle_out,
    query_out,
    pair_out,
    grads_out,
    query_grad,
    key_grad,
):
    width = query_ref.shape[1]
    rows = query_ref.shape[0]
    grad_norm, _ = norm_backward(
        part_ref[...] + other_ref[...], centered_ref[...], inverse_ref[...], gain_ref[...]
    )
    grad_middle = back_ref[...].astype(F32) + grad_norm
    middle_out[...] = grad_middle
    middle_low = grad_middle.astype(BF16)
    grad_attended = kernel_dot(middle_low, weight_ref[:, :width], 1, 0).astype(BF16)
    keep = keep_ref[...] > 0
    for head in range(width // HEAD):
        at = slice(HEAD * head, HEAD * (head + 1))
        value_at = slice(width + HEAD * head, width + HEAD * (head + 1))
        query, grad = query_ref[:, at] * HEAD ** (-0.5), grad_attended[:, at]
        key, value = pair_ref[:, at], pair_ref[:, value_at]
        probs = softmax_turned(keep, key, query)
        grad_probs = kernel_dot(value, grad, 1, 1)
        centre = jnp.sum(probs * grad_probs, axis=0, keepdims=True)
        grad_raw = (probs * (grad_probs - centre)).astype(BF16)
        query_grad[:, at] = kernel_dot(grad_raw, key, 0, 0) * HEAD ** (-0.5)
        key_grad[:, at] = kernel_dot(grad_raw, query, 1, 0)
        pair_out[:, value_at] = kernel_dot(probs.astype(BF16), grad, 1, 0).astype(BF16)

    def unrotated(values, count):
        return (values * cosine_ref[:count] - turned(values) * sine_ref[:count]).astype(BF16)

    for start in range(0, width, LANE):
        at = slice(start, start + LANE)
        query_out[:, at] = unrotated(query_grad[:, at], rows)
        pair_out[:, at] = unrotated(key_grad[:, at], key_grad.shape[0])
    normed = normed_ref[...]
    put_by_z(kernel_dot(normed, pair_out[...], 0, 0).astype(BF16), grads_out, 0)
    put_by_z(
        kernel_dot(normed[:rows], query_out[...], 0, 0).astype(BF16), grads_out, 2 * width
    )
    put_by_z(kernel_dot(middle_low, attended_ref[...], 0, 0).astype(BF16), grads_out, 3 * width)


def on_device(
    tokens,
    cotangent,
    lengths,
    assign,
    norm_gains,
    project_weight,
    output_weight,
    expand_weight,
    shrink_weight,
    norm_first,
    norm_second,
    project_first,
    project_second,
    output_first,
    output_second,
    expand_first,
    expand_second,
    shrink_first,
    shrink_second,
):
    row, col = lax.axis_index("row"), lax.axis_index("col")
    shard_rows = project_weight.shape[0]
    output_width = output_weight.shape[0]
    expand_width = 2 * expand_weight.shape[2]
    shrink_width = shrink_weight.shape[0]
    heads_here = output_width // HEAD

    slot = (lax.axis_index("xh") * 4 + lax.axis_index("z")) * 2 + (col >> 1)
    catalog = jnp.arange(lengths.shape[0], dtype=jnp.int32)
    seq_id = jnp.sum(jnp.where(catalog == slot, assign, 0))
    slot_length = jnp.sum(jnp.where(catalog == seq_id, lengths, 0))
    block_rows = tokens.shape[1] // 2
    within = jnp.arange(block_rows, dtype=jnp.int32)

    def block_positions(flip_row, flip_col):
        return (2 * (row ^ flip_row) + ((col & 1) ^ flip_col)) * block_rows + within

    positions = block_positions(0, 0)
    key_pos = jnp.concatenate([positions] + [block_positions(*flips) for flips in SQUARE])
    keep = (key_pos < slot_length)[:, None].astype(jnp.int32)
    cosine, sine = rotary_tables(key_pos)

    head_width = output_width
    rest_width = expand_width + shrink_width
    rest_pad = -rest_width % LANE
    first_width = 3 * head_width + LANE
    middle_width = head_width + expand_width
    shard = jnp.concatenate(
        [
            project_weight[:, 1],
            norm_gains.T,
            jnp.zeros((shard_rows, LANE - 2), F32),
            project_weight[:, 0],
            project_weight[:, 2],
            output_weight.T,
            expand_weight.reshape(shard_rows, expand_width),
            shrink_weight.T,
            jnp.zeros((shard_rows, rest_pad), F32),
        ],
        axis=1,
    ).astype(BF16)
    columns = tokens.shape[2]
    arrived = to_chip(jnp.concatenate([tokens[0], cotangent[0]], axis=1))
    block = gather_x(shard)
    first_pieces = ring_pieces(block[:, :first_width], "z")
    rest_pieces = ring_pieces(block[:, first_width:], "col")
    stages = together(*first_pieces, *rest_pieces)
    first_pieces = ring_halves(jnp.stack(stages[:4]), "col")
    rest_gathered = lax.all_gather(jnp.stack(stages[4:]), "z")
    tokens_own = jnp.concatenate([piece[:, :columns] for piece in arrived], axis=1)
    tokens_half = [tokens_own] + [square_move(tokens_own, *flips) for flips in SQUARE]
    cotangent_own = jnp.concatenate([piece[:, columns:] for piece in arrived], axis=1)
    tokens_all = join_cores(jnp.concatenate(tokens_half))
    cotangent_chip = join_cores(cotangent_own)
    back = jnp.where(
        (positions < slot_length)[:, None], cotangent_chip, jnp.zeros_like(cotangent_chip)
    )
    centered_all, inverse_all = norm_forward(tokens_all.astype(F32))
    inputs = tokens_all[:block_rows]
    centered_one, inverse_one = centered_all[:block_rows], inverse_all[:block_rows]

    features = tokens_all.shape[1]
    keys_count = tokens_all.shape[0]
    place = jnp.stack([col, lax.axis_index("z")]).astype(jnp.int32)
    first_all, gains_low, normed_all, queries, pairs, attended = kernel_call(
        forward_kernel,
        [
            ((4, 2, 4, features // 32, first_width), BF16),
            ((8, features), F32),
            ((keys_count, features), BF16),
            ((block_rows, head_width), BF16),
            ((keys_count, 2 * head_width), BF16),
            ((block_rows, head_width), BF16),
        ],
        place,
        *first_pieces,
        keep,
        centered_all,
        cosine,
        sine,
        scalars=1,
        grant=WIDE_GRANT,
    )
    first_all = first_all.reshape(features, first_width)
    gain_one, gain_two = gains_low[:1], gains_low[1:2]
    key_low = first_all[:, :head_width]
    query_low = first_all[:, head_width + LANE : 2 * head_width + LANE]
    value_low = first_all[:, 2 * head_width + LANE :]
    middle_all, shrink_all, output_part = kernel_call(
        output_kernel,
        [
            ((4, 2, 4, features // 32, middle_width), BF16),
            ((4, 2, 4, features // 32, shrink_width + rest_pad), BF16),
            ((block_rows, features), F32),
        ],
        place,
        attended,
        rest_gathered,
        scalars=1,
    )
    middle_all = middle_all.reshape(features, -1)
    shrink_all = shrink_all.reshape(features, -1)
    centered_two, inverse_two, normed_two, hidden, grad_expanded, mixed_part, normed_grad_part = (
        kernel_call(
            feed_kernel,
            [
                ((block_rows, features), F32),
                ((block_rows, 1), F32),
                ((block_rows, features), BF16),
                ((block_rows, shrink_width), BF16),
                ((block_rows, expand_width), BF16),
                ((block_rows, features), F32),
                ((block_rows, features), F32),
            ],
            inputs,
            output_part,
            swap_cores(output_part),
            gain_two,
            middle_all,
            shrink_all,
            back,
        )
    )
    normed_grad_other = swap_cores(normed_grad_part)
    (rest_grad,) = kernel_call(
        rest_grads_kernel,
        [((4, 8, features // 32, rest_width + rest_pad), BF16)],
        normed_two,
        grad_expanded,
        back,
        hidden,
    )
    rest_own = lax.psum_scatter(
        rest_grad.reshape(features, -1), "z", scatter_dimension=0, tiled=True
    )
    normed_grad_other, rest_grad = together(normed_grad_other, rest_grad)
    grad_mid, query_grad, pair_grad, first_grad = kernel_call(
        backward_kernel,
        [
            ((block_rows, features), F32),
            ((block_rows, head_width), BF16),
            ((keys_count, 2 * head_width), BF16),
            ((4, 8, features // 32, 4 * head_width), BF16),
        ],
        keep,
        normed_grad_part,
        normed_grad_other,
        centered_two,
        inverse_two,
        gain_two,
        back,
        middle_all,
        queries,
        pairs,
        normed_all,
        attended,
        cosine,
        sine,
        scratch=[((block_rows, head_width), F32), ((keys_count, head_width), F32)],
        grant=WIDE_GRANT,
    )
    first_sum = exchange_sum(first_grad.reshape(4, features // 4, -1), "z")
    parts = pair_grad.reshape(4, block_rows, 2 * head_width)
    received = [square_move(parts[index + 1], *flips) for index, flips in enumerate(SQUARE)]
    rest_own, *received = together(rest_own, *received)
    rest_sum = scatter_col(rest_own).astype(BF16)
    first_sum, rest_sum, mixed_part = together(first_sum, rest_sum, mixed_part)
    received = together(first_sum, *received)[1:]
    first_sum = exchange_sum(first_sum.reshape(4, features // 16, -1), "col")
    owned_part = jnp.concatenate([first_sum, rest_sum], axis=1)
    pair_total = sum((piece.astype(F32) for piece in received), parts[0].astype(F32))
    pair_total = pair_total.astype(BF16)

    grad_normed_one = sum_cores(
        product_turned(query_grad, query_low)
        + product_turned(pair_total[:, :head_width], key_low)
        + product_turned(pair_total[:, head_width:], value_low)
    )
    grad_input_norm, _ = norm_backward(grad_normed_one, centered_one, inverse_one, gain_one)
    grad_input_chip = (grad_mid + grad_input_norm).astype(BF16)
    mixed_chip = sum_cores(mixed_part).astype(BF16)
    owned_part, grad_input_chip, mixed_chip = together(owned_part, grad_input_chip, mixed_chip)
    owned = scatter_x(owned_part)
    mixed_home, grad_input = from_chip(mixed_chip, grad_input_chip)

    project_grad = jnp.stack(
        [
            owned[:, 2 * head_width : 3 * head_width],
            owned[:, :head_width],
            owned[:, head_width : 2 * head_width],
        ],
        axis=1,
    )
    first_owned, rest_owned = owned[:, 3 * head_width :], owned[:, 4 * head_width :]

    def gain_part(weight, grad):
        return jnp.sum(weight.astype(BF16).astype(F32) * grad, axis=(1, 2))

    expand_grad = rest_owned[:, :expand_width].reshape(expand_weight.shape)
    gain_grad = jnp.stack(
        [gain_part(project_weight, project_grad), gain_part(expand_weight, expand_grad)]
    )
    gain_grad = gain_grad + move(gain_grad, ("row",), lambda place: (place ^ 1,))
    gain_grad = gain_grad / norm_gains.astype(BF16).astype(F32)
    output_grad = first_owned[:, :output_width].T
    shrink_grad = rest_owned[:, expand_width:rest_width].T
    return (
        (mixed_home[None], grad_input[None])
        + adam_update(norm_gains, gain_grad, norm_first, norm_second, rate_gain, 0.0)
        + adam_update(
            project_weight, project_grad, project_first, project_second, rate_matrix, decay_matrix
        )
        + adam_update(
            output_weight, output_grad, output_first, output_second, rate_matrix, decay_matrix
        )
        + adam_update(
            expand_weight, expand_grad, expand_first, expand_second, rate_matrix, decay_matrix
        )
        + adam_update(
            shrink_weight, shrink_grad, shrink_first, shrink_second, rate_matrix, decay_matrix
        )
    )


def solution(mesh):
    fine = Mesh(mesh.devices.reshape(tuple(SIZES.values())), tuple(SIZES))
    dp = ("xh", "z", "core")
    owners = ("col",) + dp
    active = P(dp, "row", "col")
    gains = P(None, owners)
    features_first = P(owners, None, "row")
    features_last = P("row", owners)
    params = (gains, features_first, features_last, features_first, features_last)
    moments = tuple(spec for spec in params for _ in range(2))
    results = tuple(spec for spec in params for _ in range(4))
    return jax.shard_map(
        on_device,
        mesh=fine,
        in_specs=(active, active, P(), P()) + params + moments,
        out_specs=(active, active) + results,
        check_vma=False,
    )
```
